128 devices in a mesh: resp: 8 (over z, core), expert: 4 (over x), prompt: 4 (over y).
Axes of the slice: x: 4, y: 4, z: 4, core: 2. Of those that a mesh axis runs over, the one named last changes fastest.
Arguments:
- hidden: bfloat16 [256, 7168], P(('prompt', 'resp'), 'expert'), parts along dimension 0, may hold values from -6 to 6
- queries: bfloat16 [256, 128, 576], P(('prompt', 'resp'), 'expert'), parts along dimension 0, may hold values from -128 to 128
- new_latents: bfloat16 [256, 576], P(('prompt', 'resp')), parts along dimension 0, may hold values from -6 to 6
- suffix_cache: bfloat16 [64, 512, 576], P(('prompt', 'resp')), parts along dimension 0, may hold values from -6 to 6
- suffix_lengths: int32 [64], P(('prompt', 'resp')), parts along dimension 0, may hold values from 1 to 512, 6144 in all
- prompt_latents: bfloat16 [131072, 576], P(('prompt', 'resp', 'expert')), parts along dimension 0, may hold values from -6 to 6
- value_up: bfloat16 [128, 512, 128], P('expert'), may hold values from -0.25 to 0.25
- out_proj: bfloat16 [128, 128, 7168], P('expert', 'resp'), may hold values from -0.0625 to 0.0625
- rms_gain: float32 [7168], replicated, may hold values from 0.1 to 1.9
- gate_ids: int32 [256, 2], P('prompt'), parts along dimension 0, may hold values from 0 to 3, all different within a row
- gate_weights: float32 [256, 2], P('prompt'), parts along dimension 0, may hold values from 0.1 to 1
- w_gate: bfloat16 [4, 7168, 2048], P('expert', None, 'resp'), may hold values from -0.0625 to 0.0625
- w_up: bfloat16 [4, 7168, 2048], P('expert', None, 'resp'), may hold values from -0.0625 to 0.0625
- w_down: bfloat16 [4, 2048, 7168], P('expert', 'resp'), may hold values from -0.1875 to 0.1875
Outputs:
- attended: bfloat16 [256, 7168], P(('prompt', 'resp'), 'expert'), parts along dimension 0
- layer_out: bfloat16 [256, 7168], P(('prompt', 'resp'), 'expert'), parts along dimension 0
The draws below stay inside these ranges and needn't reach their ends.
There are 4 independent parts, one for each index of `prompt`. The reference program is written for one: setup_inputs(seed, part) draws one part's arguments, and reference() takes and returns one part's arrays. A program takes and returns all parts, laid end to end along the dimension named above; an argument that names none is the same for every part. Nothing has to cross between parts.
Inputs may be any that keep to these rules, and one draw needn't show every extreme that they name: `suffix_lengths`: each response has 1 to 512 live cache slots; some response has exactly 512. `gate_ids`: each token names 2 different experts.
All inputs are finite; a program needn't handle non-finite values. No bound on the sum of `suffix_lengths` on one device may be relied on, other than what follows from the above.
Results may differ from the reference program's by a relative error of at most 0.03.
Values may be sent and summed in bfloat16 or wider, within the bound.
A program may use at most 256 MiB of HBM per device.

```python
import math
import jax
import jax.numpy as jnp
import numpy as np
from jax import lax

D = 7168
HEADS = 128
LAT = 512
ROPE = 64
NOPE = 128
VDIM = 128
FF = 2048
LATK = 576
STEPS = 4
TOPK = 2
SUF = 512
RESPONSES = 16
TOKENS = 64
PROMPT = 32768
EXPERTS = 4


def shared_latents(key):
    first_key, second_key, third_key = jax.random.split(key, 3)
    prompt_rows = jnp.clip(jax.random.normal(first_key, (PROMPT, LATK), jnp.float32), -6.0, 6.0)
    fresh_rows = jnp.clip(jax.random.normal(second_key, (TOKENS, LATK), jnp.float32), -6.0, 6.0)
    cache_rows = jnp.clip(jax.random.normal(third_key, (RESPONSES, SUF, LATK), jnp.float32), -6.0, 6.0)
    return (prompt_rows, fresh_rows, cache_rows)


def draw_prompt_latents(key, part):
    prompt_rows, fresh_rows, cache_rows = shared_latents(key)
    return prompt_rows.astype(jnp.bfloat16)


def draw_new_latents(key, part):
    prompt_rows, fresh_rows, cache_rows = shared_latents(key)
    return fresh_rows.astype(jnp.bfloat16)


def draw_suffix_cache(key, part):
    prompt_rows, fresh_rows, cache_rows = shared_latents(key)
    return cache_rows.astype(jnp.bfloat16)


def draw_queries(key, part):
    prompt_rows, fresh_rows, cache_rows = shared_latents(key)
    key = jax.random.fold_in(key, 3)
    factor = (NOPE + ROPE) ** (-0.5)
    spread = 3.0 / (factor * LATK ** 0.5)
    pull = 14.0 / (factor * LATK)
    cache_pull = 3.0 * SUF / (factor * LATK)
    noise = jax.random.normal(key, (TOKENS, HEADS, LATK), jnp.float32)
    cache_mean = jnp.repeat(jnp.mean(cache_rows, axis=1), STEPS, axis=0)
    result = spread * noise + pull * fresh_rows[:, None, :] + cache_pull * cache_mean[:, None, :]
    return jnp.clip(result, -128.0, 128.0).astype(jnp.bfloat16)


def strengthened(drawn, rng, source, target, parts, factor):
    def block_of(dim):
        return (jnp.arange(drawn.shape[dim]) // (drawn.shape[dim] // parts)).reshape((-1,) + (1,) * (drawn.ndim - 1 - dim))

    near = jax.random.permutation(rng, parts)[block_of(target)]
    other_side = (block_of(target) + parts // 2) % parts
    return jnp.where((block_of(source) == near) | (block_of(source) == other_side), factor * drawn, drawn)


def block_scale(own_key, dims, cuts, least, largest):
    gain = 1.0
    for axis_at, parts in cuts:
        steps = jax.random.uniform(jax.random.fold_in(jax.random.fold_in(own_key, 6), axis_at), (parts,), jnp.float32, least / len(cuts), largest / len(cuts))
        gain = gain * jnp.repeat(jnp.exp(steps), dims[axis_at] // parts).reshape((-1,) + (1,) * (len(dims) - 1 - axis_at))
    return gain


def choose_distinct(stream_key, rows, number_of, top, lift):
    sequence = jax.random.permutation(jax.random.fold_in(stream_key, 1), number_of)
    favour = sequence
    for power in range(3):
        favour = favour * favour // number_of
    favour = favour * lift // number_of
    tickets = jax.random.randint(jax.random.fold_in(stream_key, 2), (rows, number_of), 0, 4096) + favour
    sure = jax.random.permutation(jax.random.fold_in(stream_key, 3), rows)[jnp.arange(number_of) % rows]
    tickets = jnp.where(jnp.arange(rows)[:, None] == sure[None, :], 1 << 14, tickets)
    score = tickets * number_of + jnp.arange(number_of)
    return lax.top_k(score.astype(jnp.int32), top)[1].astype(jnp.int32)


def profile(amount, total, most, skew):
    loads = [(1 << 20) // math.isqrt(grade ** skew) + 1 for grade in range(2, amount + 1)]
    surplus, holding = total - most - (amount - 1), [1] * (amount - 1)
    while surplus > 0:
        movable = [i for i in range(amount - 1) if holding[i] < most]
        mass, budget = sum([loads[i] for i in movable]), surplus
        for i in movable:
            addition = min(most - holding[i], max(1, budget * loads[i] // mass), surplus)
            holding[i] = holding[i] + addition
            surplus = surplus - addition
    return np.array([most] + holding)


def ragged_sizes(key, amount, total, bound, slope):
    if amount == 2:
        one = jax.random.randint(key, (), max(1, total - bound), min(bound, total - 1) + 1)
        return jnp.stack([one, total - one])
    lengths = jnp.asarray(profile(amount, total, bound, slope), jnp.int32)
    twos = (amount - 1) // 2
    source_of, sink = lengths[1:1 + 2 * twos:2], lengths[2:2 + 2 * twos:2]
    slack = jnp.minimum(source_of - 1, bound - sink)
    moved = jax.random.randint(jax.random.fold_in(key, 1), (twos,), 0, 1 << 20) % (slack + 1)
    lengths = lengths.at[1:1 + 2 * twos:2].set(source_of - moved).at[2:2 + 2 * twos:2].set(sink + moved)
    return lengths[jax.random.permutation(jax.random.fold_in(key, 2), amount)]


def gaussian(key, shape, width, limit, pieces=(), held_as=jnp.bfloat16):
    loudness = block_scale(key, shape, pieces, -0.22, 0.18) if pieces else 1.0
    values = jax.random.normal(key, shape, jnp.float32) * width * loudness
    return jnp.minimum(jnp.maximum(values, -limit), limit).astype(held_as)


def noise_with(stream_key, shape, width, reach, cuts, heavy, kind=jnp.bfloat16):
    values = width * jax.random.normal(stream_key, shape, jnp.float32)
    if cuts:
        values = values * block_scale(stream_key, shape, cuts, -0.22, 0.18)
    return jnp.clip(strengthened(values, jax.random.fold_in(stream_key, 3), *heavy), -reach, reach).astype(kind)


def setup_inputs(seed: int = 0, part: int = 0) -> dict:
    streams_of = jax.random.split(jax.random.key(seed), 15)
    part_keys = jax.random.split(jax.random.fold_in(streams_of[14], part), 15)
    hidden = gaussian(part_keys[0], (TOKENS, D), 1.0, 6.0, ((0, 8), (1, 4)))
    queries = draw_queries(jax.random.fold_in(jax.random.fold_in(streams_of[14], part), 71), part)
    new_latents = draw_new_latents(jax.random.fold_in(jax.random.fold_in(streams_of[14], part), 71), part)
    suffix_cache = draw_suffix_cache(jax.random.fold_in(jax.random.fold_in(streams_of[14], part), 71), part)
    suffix_lengths = ragged_sizes(part_keys[4], RESPONSES, (3 * SUF * RESPONSES) // 4, SUF, 1).astype(jnp.int32)
    prompt_latents = draw_prompt_latents(jax.random.fold_in(jax.random.fold_in(streams_of[14], part), 71), part)
    value_up = gaussian(streams_of[6], (HEADS, LAT, VDIM), LAT ** -0.5, 0.25, ((0, 4),))
    out_proj = noise_with(streams_of[7], (HEADS, VDIM, D), (HEADS * VDIM) ** -0.5, 0.0625, ((0, 4), (1, 8)), (0, 2, 4, 2.0))
    rms_gain = jnp.clip(1.0 + 0.18 * jax.random.normal(streams_of[8], (D,), jnp.float32), 0.1, 1.9)
    gate_ids = choose_distinct(part_keys[9], TOKENS, EXPERTS, TOPK, 4096)
    gate_weights = jnp.clip(jnp.exp(jax.random.uniform(part_keys[10], (TOKENS, TOPK), jnp.float32, math.log(0.1), math.log(1.0))), 0.1, 1.0)
    w_gate = gaussian(streams_of[11], (EXPERTS, D, FF), D ** -0.5, 0.0625, ((0, 4), (2, 8)))
    w_up = gaussian(streams_of[12], (EXPERTS, D, FF), D ** -0.5, 0.0625, ((0, 4), (2, 8)))
    w_down = noise_with(streams_of[13], (EXPERTS, FF, D), FF ** -0.5, 0.1875, ((0, 4), (1, 8)), (1, 2, 8, 2.0))
    return dict(hidden=hidden, queries=queries, new_latents=new_latents, suffix_cache=suffix_cache, suffix_lengths=suffix_lengths, prompt_latents=prompt_latents, value_up=value_up, out_proj=out_proj, rms_gain=rms_gain, gate_ids=gate_ids, gate_weights=gate_weights, w_gate=w_gate, w_up=w_up, w_down=w_down)


def reference(hidden, queries, new_latents, suffix_cache, suffix_lengths, prompt_latents, value_up, out_proj, rms_gain, gate_ids, gate_weights, w_gate, w_up, w_down):
    factor = (NOPE + ROPE) ** (-0.5)

    def one_response(index):
        query_rows = lax.dynamic_slice_in_dim(queries, index * STEPS, STEPS, 0).reshape(STEPS * HEADS, LATK)
        cache = lax.dynamic_index_in_dim(suffix_cache, index, 0, keepdims=False)
        fresh_keys = lax.dynamic_slice_in_dim(new_latents, index * STEPS, STEPS, 0)
        length = lax.dynamic_index_in_dim(suffix_lengths, index, 0, keepdims=False)
        far_scores = jnp.dot(query_rows, prompt_latents.T, preferred_element_type=jnp.float32) * factor
        cache_scores = jnp.dot(query_rows, cache.T, preferred_element_type=jnp.float32) * factor
        own_scores = jnp.dot(query_rows, fresh_keys.T, preferred_element_type=jnp.float32) * factor
        cache_live = (jnp.arange(SUF, dtype=jnp.int32) < length)[None, :]
        row_step = jnp.arange(STEPS * HEADS, dtype=jnp.int32) // HEADS
        own_live = jnp.arange(STEPS, dtype=jnp.int32)[None, :] <= row_step[:, None]
        cache_scores = jnp.where(cache_live, cache_scores, -jnp.inf)
        own_scores = jnp.where(own_live, own_scores, -jnp.inf)
        highest = jnp.maximum(lax.optimization_barrier(jnp.max(far_scores, axis=1)), jnp.maximum(lax.optimization_barrier(jnp.max(cache_scores, axis=1)), lax.optimization_barrier(jnp.max(own_scores, axis=1))))[:, None]
        far_exp = jnp.exp(far_scores - highest)
        cache_exp = jnp.exp(cache_scores - highest)
        own_exp = jnp.exp(own_scores - highest)
        denom = lax.optimization_barrier(jnp.sum(far_exp, axis=1)) + lax.optimization_barrier(jnp.sum(cache_exp, axis=1)) + lax.optimization_barrier(jnp.sum(own_exp, axis=1))
        denom = denom[:, None]
        context = jnp.dot((far_exp / denom).astype(jnp.bfloat16), prompt_latents[:, :LAT], preferred_element_type=jnp.float32)
        context = context + jnp.dot((cache_exp / denom).astype(jnp.bfloat16), cache[:, :LAT], preferred_element_type=jnp.float32)
        context = context + jnp.dot((own_exp / denom).astype(jnp.bfloat16), fresh_keys[:, :LAT], preferred_element_type=jnp.float32)
        return context.astype(jnp.bfloat16).reshape(STEPS, HEADS, LAT)
    context = lax.map(one_response, jnp.arange(RESPONSES, dtype=jnp.int32)).reshape(TOKENS, HEADS, LAT)
    head_values = jnp.einsum('thc,hcv->thv', context.astype(jnp.float32), value_up.astype(jnp.float32)).astype(jnp.bfloat16)
    attended = jnp.dot(head_values.reshape(TOKENS, HEADS * VDIM), out_proj.reshape(HEADS * VDIM, D), preferred_element_type=jnp.float32).astype(jnp.bfloat16)
    resid = (hidden.astype(jnp.float32) + attended.astype(jnp.float32)).astype(jnp.bfloat16)
    resid_wide = resid.astype(jnp.float32)
    mean_square = lax.optimization_barrier(jnp.mean(resid_wide * resid_wide, axis=1, keepdims=True))
    normed = (resid_wide * lax.rsqrt(mean_square + 1e-06) * rms_gain[None, :]).astype(jnp.bfloat16)
    picked = (gate_ids[:, :, None] == jnp.arange(EXPERTS, dtype=jnp.int32)[None, None, :]).astype(jnp.float32)
    coef = 2.5 * lax.optimization_barrier(jnp.sum(gate_weights[:, :, None] * picked, axis=1)) / lax.optimization_barrier(jnp.sum(gate_weights, axis=1, keepdims=True))

    def one_expert(moe_sum, weights):
        gate_part, up_part, down_part, share = weights
        gate_value = jnp.dot(normed, gate_part, preferred_element_type=jnp.float32)
        up_value = jnp.dot(normed, up_part, preferred_element_type=jnp.float32)
        activation = (jax.nn.silu(gate_value) * up_value).astype(jnp.bfloat16)
        expert_out = jnp.dot(activation, down_part, preferred_element_type=jnp.float32)
        return (moe_sum + share[:, None] * expert_out, None)
    moe, ignored = lax.scan(one_expert, jnp.zeros((TOKENS, D), jnp.float32), (w_gate, w_up, w_down, coef.T))
    layer_out = (resid.astype(jnp.float32) + moe).astype(jnp.bfloat16)
    return (attended, layer_out)
```

```python
import jax
import jax.numpy as jnp
from jax import lax
from jax.experimental import pallas as pl
from jax.experimental.pallas import tpu as pltpu
from jax.sharding import PartitionSpec as P

MESH = pl.DeviceIdType.MESH
BF = jnp.bfloat16
F32 = jnp.float32
LAT, ROPE, LATK = 512, 64, 576
SCALE2 = (128 + 64) ** -0.5 * 1.4426950408889634
FLOOR = -0.5e30
DEAD = -1e30
D = 7168
HALF = 896
KC = 256
GROUP = 512


def iota(shape, dim):
    return lax.broadcasted_iota(jnp.int32, shape, dim)


def dot(a, b):
    return jnp.dot(a, b, preferred_element_type=F32)


def kernel(
    slen,
    hid,
    newl,
    gain,
    gids,
    gwts,
    q_in,
    k_in,
    suf_in,
    vup_in,
    wo_in,
    wg_in,
    wu_in,
    wd_in,
    att_out,
    layer_out,
    q_all,
    qt,
    k_own,
    k_all,
    rope,
    kt_own,
    kt,
    suf,
    nl,
    acc,
    mx,
    sm,
    vup,
    wo,
    wg,
    wu,
    wd,
    ctx,
    hv,
    hv_tx,
    hv_rx,
    st_rx,
    a_buf,
    a_rx,
    a_sum,
    a_in,
    ag,
    m_buf,
    m_rx,
    m_sum,
    m_in,
    ld,
    kss,
    krs,
    rss,
    rrs,
    qss,
    qrs,
    qcs,
    qcr,
    hss,
    hrs,
    tss,
    trs,
    acs,
    acr,
    ars_s,
    ars_r,
    ags_s,
    ags_r,
    agc_s,
    agc_r,
    mcs,
    mcr,
    mrs_s,
    mrs_r,
):
    e = lax.axis_index("expert")
    r = lax.axis_index("resp")
    c = lax.rem(r, 2)
    z = r // 2
    right, left = lax.rem(e + 1, 4), lax.rem(e + 3, 4)
    twin = {"resp": z * 2 + 1 - c}

    def remote(src, dst, ssem, rsem, dev):
        return pltpu.make_async_remote_copy(
            src_ref=src, dst_ref=dst, send_sem=ssem, recv_sem=rsem, device_id=dev, device_id_type=MESH
        )

    def same_core(de, dz):
        return {"expert": lax.rem(e + de, 4), "resp": lax.rem(z + dz, 4) * 2 + c}

    loads = [
        pltpu.make_async_copy(q_in, q_all.at[r], ld.at[0]),
        pltpu.make_async_copy(k_in, k_own, ld.at[1]),
        pltpu.make_async_copy(suf_in, suf, ld.at[2]),
        pltpu.make_async_copy(vup_in, vup, ld.at[3]),
        pltpu.make_async_copy(wo_in, wo, ld.at[4]),
        pltpu.make_async_copy(wg_in, wg, ld.at[5]),
        pltpu.make_async_copy(wu_in, wu, ld.at[6]),
        pltpu.make_async_copy(wd_in, wd, ld.at[7]),
    ]
    for x in loads[:3]:
        x.start()

    bar = pltpu.get_barrier_semaphore()
    for i in range(1, 16):
        pl.semaphore_signal(bar, inc=1, device_id=same_core(i % 4, i // 4), device_id_type=MESH)
    for i in range(4):
        pl.semaphore_signal(
            bar,
            inc=1,
            device_id={"resp": lax.rem(z + i, 4) * 2 + 1 - c},
            device_id_type=MESH,
        )
    pl.semaphore_wait(bar, 19)

    def k_send(src, j, d):
        slot = 4 + 2 * j + d
        dev = {"expert": right if d == 0 else left}
        return remote(src, k_all.at[slot], kss.at[2 * j + d], krs.at[2 * j + d], dev)

    def rope_send(src, j, d):
        slot = 4 + 2 * j + d
        dev = {"expert": right if d == 0 else left}
        return remote(rope.at[src], rope.at[slot], rss.at[2 * j + d], rrs.at[2 * j + d], dev)

    def own_chunk(j, d):
        return j if d == 0 else 3 - j

    k_own_sends = [
        k_send(k_in.at[pl.ds(KC * own_chunk(j, d), KC), pl.ds(0, LAT)], j, d)
        for j in range(4)
        for d in range(2)
    ]
    rope_own_sends = [rope_send(own_chunk(j, d), j, d) for j in range(4) for d in range(2)]

    def q_send(i):
        return remote(q_in, q_all.at[r], qss.at[i], qrs.at[i], same_core(0, i))

    def q_cross(i):
        src = lax.rem(z + 4 - i, 4) * 2 + c
        return remote(q_all.at[src], q_all.at[src], qcs.at[i], qcr.at[i], twin)

    own_q_cross = remote(q_in, q_all.at[r], qcs.at[0], qcr.at[0], twin)
    own_q_cross.start()
    for x in k_own_sends[:2]:
        x.start()
    for i in (1, 3, 2):
        q_send(i).start()
    for x in k_own_sends[2:]:
        x.start()

    mx[...] = jnp.full_like(mx, FLOOR)
    sm[...] = jnp.zeros_like(sm)
    acc[...] = jnp.zeros_like(acc)
    nl[...] = jnp.zeros_like(nl)
    nl[0:8, :] = newl[...]

    loads[1].wait()
    rope_t = k_own[:, LAT:LATK].T
    for i in range(4):
        rope[i] = rope_t[:, KC * i : KC * (i + 1)]
    for x in rope_own_sends:
        x.start()
    for b in range(2):
        kt_own[b] = k_own[GROUP * b : GROUP * (b + 1), :LAT].T

    def soft(s, g, vt):
        old = mx[g]
        new = jnp.maximum(old, jnp.max(s, axis=0, keepdims=True))
        mx[g] = new
        p = jnp.exp2((s - new) * SCALE2)
        shrink = jnp.exp2((old - new) * SCALE2)
        sm[g] = sm[g] * shrink + jnp.sum(p, axis=0, keepdims=True)
        acc[g] = acc[g] * shrink + dot(vt, p.astype(BF))

    def make_qt(g):
        block = q_all[pl.ds(2 * g, 2)].reshape(GROUP, LATK)
        row, col = iota((GROUP, GROUP), 0), iota((GROUP, GROUP), 1)
        want = ((col // 8) % 2) * 256 + (col % 8) * 32 + col // 16
        place = jnp.where(row == want, 1.0, 0.0).astype(BF)
        qt[g] = dot(block.T, place).astype(BF)

    def own_keys(g):
        s0 = dot(k_own[0:GROUP, :], qt[g])
        s1 = dot(k_own[GROUP : 2 * GROUP, :], qt[g])
        soft(s0, g, kt_own[0])
        soft(s1, g, kt_own[1])

    loads[0].wait()
    own_q_cross.wait_recv()
    make_qt(z)
    loads[2].wait()
    for x in loads[3:]:
        x.start()
    tok = iota((1, GROUP), 1) % 16
    mine = (tok // 8) == c
    for b in range(2):
        rows = suf[GROUP * b : GROUP * (b + 1), :]
        s = dot(rows, qt[z])
        live = (iota((GROUP, GROUP), 0) < slen[b]) & mine & ((tok % 8) // 4 == b)
        kt[...] = rows[:, :LAT].T
        soft(jnp.where(live, s, DEAD), z, kt[...])
    s = dot(nl[...], qt[z])
    key = iota((128, GROUP), 0)
    live = (key < 8) & mine & ((tok % 8) // 4 == key // 4) & (key % 4 <= tok % 4)
    soft(jnp.where(live, s, DEAD), z, nl[:, :LAT].T)
    own_keys(z)

    for i in (1, 3, 2):
        q_send(i).wait_recv()
        q_cross(i).start()
    for i in (1, 3, 2):
        g = lax.rem(z + 4 - i, 4)
        q_cross(i).wait_recv()
        make_qt(g)
        own_keys(g)

    def pair(j, forward):
        for d in range(2):
            slot = 4 + 2 * j + d
            k_send(k_all.at[slot], j, d).wait_recv()
            rope_send(slot, j, d).wait_recv()
            if forward:
                k_send(k_all.at[slot], j + 4, d).start()
                rope_send(slot, j + 4, d).start()
        kn = k_all[pl.ds(4 + 2 * j, 2)].reshape(GROUP, LAT)
        rp = jnp.concatenate([rope[4 + 2 * j].T, rope[5 + 2 * j].T], axis=0)
        kt[...] = kn.T

        def score(g):
            return dot(kn, qt[g, 0:LAT, :]) + dot(rp, qt[g, LAT:LATK, :])

        s = score(0)
        for g in range(4):
            nxt = score(g + 1) if g < 3 else None
            soft(s, g, kt[...])
            s = nxt

    def pair_forward(j, carry):
        pair(j, True)
        return carry

    def pair_last(j, carry):
        pair(j, False)
        return carry

    lax.fori_loop(0, 2, pair_forward, 0)
    lax.fori_loop(2, 6, pair_last, 0)

    for g in range(4):
        part = (acc[g] * (1.0 / sm[g])).astype(BF)
        ctx[:, g] = part.T.reshape(32, 16, LAT)
    loads[3].wait()

    def project(h, carry):
        hv[h] = dot(ctx[h].reshape(64, LAT), vup[h]).reshape(4, 16, 128)
        return carry

    lax.fori_loop(0, 32, project, 0, unroll=4)
    for g in range(4):
        for hb in range(4):
            block = hv[8 * hb : 8 * hb + 8, g].reshape(128, 128).T.astype(BF)
            hv_tx[:, :, GROUP * g + 128 * hb : GROUP * g + 128 * hb + 128] = block.reshape(8, 16, 128)
        st_rx[0, 0:1, GROUP * g : GROUP * (g + 1)] = mx[g]
        st_rx[0, 1:2, GROUP * g : GROUP * (g + 1)] = sm[g]

    def hv_send(i):
        to = lax.rem(r + i, 8)
        return remote(hv_tx.at[to], hv_rx.at[i], hss.at[i], hrs.at[i], {"resp": to})

    def st_send(i):
        to = lax.rem(r + i, 8)
        return remote(st_rx.at[0], st_rx.at[i], tss.at[i], trs.at[i], {"resp": to})

    for i in range(1, 8):
        st_send(i).start()
        hv_send(i).start()
    for i in range(1, 8):
        st_send(i).wait_recv()
        hv_send(i).wait_recv()

    top = st_rx[0, 0:1, :]
    for i in range(1, 8):
        top = jnp.maximum(top, st_rx[i, 0:1, :])
    weights = []
    total = None
    for i in range(8):
        w = st_rx[i, 1:2, :] * jnp.exp2((st_rx[i, 0:1, :] - top) * SCALE2)
        weights.append(w)
        total = w if total is None else total + w
    inv = 1.0 / total
    y = hv_tx[r].astype(F32) * (weights[0] * inv)
    for i in range(1, 8):
        y = y + hv_rx[i].astype(F32) * (weights[i] * inv)
    y = y.astype(BF)

    col, row = iota((GROUP, 64), 1), iota((GROUP, 64), 0)
    want = ((row % 16) // 8) * 32 + (row // 128) * 8 + row % 8
    gather = jnp.where(col == want, 1.0, 0.0).astype(BF)
    keep = (iota((128, GROUP), 0) // 16) == ((iota((128, GROUP), 1) % 128) // 16)
    lhs = []
    for hb in range(4):
        piece = jnp.concatenate(
            [y[:, GROUP * g + 128 * hb : GROUP * g + 128 * hb + 128] for g in range(4)], axis=1
        )
        piece = jnp.concatenate([piece] * 8, axis=0)
        lhs.append(dot(jnp.where(keep, piece, jnp.zeros_like(piece)), gather))
    lhs = jnp.concatenate(lhs, axis=0).T.astype(BF)

    def core_send(buf, rx, ssem, rsem, x):
        return remote(buf.at[1 - c, x], rx.at[x], ssem.at[x], rsem.at[x], twin)

    def scatter_send(total_buf, landing, ssem, rsem, de, dz):
        src = total_buf.at[lax.rem(e + de, 4), lax.rem(z + dz, 4)]
        i = dz * 4 + de
        return remote(src, landing.at[i], ssem.at[i], rsem.at[i], same_core(de, dz))

    def fill(buf, x, tile):
        for cc in range(2):
            for g in range(4):
                rows = tile[32 * cc + 8 * g : 32 * cc + 8 * g + 8, :]
                buf[cc, x, g] = jnp.concatenate([rows[:, :HALF], rows[:, HALF:]], axis=0).astype(BF)

    def reduce_scatter(buf, rx, total_buf, landing, cs, cr, ss, sr):
        for de in (2, 1, 3, 0):
            x = lax.rem(e + de, 4)
            core_send(buf, rx, cs, cr, x).wait_recv()
            total_buf[x] = (buf[c, x].astype(F32) + rx[x].astype(F32)).astype(BF)
            for dz in (2, 1, 3, 0):
                if de or dz:
                    scatter_send(total_buf, landing, ss, sr, de, dz).start()
        out = total_buf[e, z].astype(F32)
        for dz in range(4):
            for de in range(4):
                if de or dz:
                    scatter_send(total_buf, landing, ss, sr, de, dz).wait_recv()
                    out = out + landing[dz * 4 + de].astype(F32)
        return out

    loads[4].wait()
    for x in range(4):
        fill(a_buf, x, dot(lhs, wo[:, 1792 * x : 1792 * (x + 1)]))
        core_send(a_buf, a_rx, acs, acr, x).start()
    attended = reduce_scatter(a_buf, a_rx, a_sum, a_in, acs, acr, ars_s, ars_r).astype(BF)
    hidden = jnp.concatenate([hid[:, :HALF], hid[:, HALF:]], axis=0)
    resid = (hidden.astype(F32) + attended.astype(F32)).astype(BF)
    ag[c, e, z] = resid
    att_out[...] = jnp.concatenate([attended[0:8], attended[8:16]], axis=1)

    def ag_send(de, dz):
        i = dz * 4 + de
        return remote(ag.at[c, e, z], ag.at[c, e, z], ags_s.at[i], ags_r.at[i], same_core(de, dz))

    def ag_cross(x):
        return remote(ag.at[c, x], ag.at[c, x], agc_s.at[x], agc_r.at[x], twin)

    for de in (0, 1, 3, 2):
        for dz in range(4):
            if de or dz:
                ag_send(de, dz).start()

    loads[5].wait()
    loads[6].wait()
    squares = jnp.zeros((64, 1), F32)
    gate = jnp.zeros((64, 256), F32)
    up = jnp.zeros((64, 256), F32)
    for de in (0, 1, 3, 2):
        x = lax.rem(e + 4 - de, 4)
        for dz in range(4):
            if de or dz:
                ag_send(de, dz).wait_recv()
        ag_cross(x).start()
    for de in (0, 1, 3, 2):
        x = lax.rem(e + 4 - de, 4)
        ag_cross(x).wait_recv()
        wide = ag[:, x].astype(F32)
        for half in range(2):
            part = wide[:, :, 8 * half : 8 * half + 8, :].reshape(64, HALF)
            squares = squares + jnp.sum(part * part, axis=1, keepdims=True)
            scaled = (part * gain[2 * x + half]).astype(BF)
            rows = pl.ds(pl.multiple_of(x * 1792 + half * HALF, HALF), HALF)
            gate = gate + dot(scaled, wg[rows, :])
            up = up + dot(scaled, wu[rows, :])
    norm = lax.rsqrt(squares * (1.0 / D) + 1e-6)
    gate = gate * norm
    up = up * norm
    act = (gate / (1.0 + jnp.exp(-gate)) * up).astype(BF)

    picked = jnp.where(gids[...] == e, gwts[...], 0.0)
    share = 2.5 * jnp.sum(picked, axis=1, keepdims=True) / jnp.sum(gwts[...], axis=1, keepdims=True)
    share = jnp.concatenate(
        [share[16 * g + 8 * cc : 16 * g + 8 * cc + 8] for cc in range(2) for g in range(4)], axis=0
    )
    loads[7].wait()
    for x in range(4):
        fill(m_buf, x, dot(act, wd[:, 1792 * x : 1792 * (x + 1)]) * share)
        core_send(m_buf, m_rx, mcs, mcr, x).start()
    moe = reduce_scatter(m_buf, m_rx, m_sum, m_in, mcs, mcr, mrs_s, mrs_r)
    out = (resid.astype(F32) + moe).astype(BF)
    layer_out[...] = jnp.concatenate([out[0:8], out[8:16]], axis=1)

    for x in k_own_sends + rope_own_sends:
        x.wait_send()
    for j in range(2):
        for d in range(2):
            slot = 4 + 2 * j + d
            k_send(k_all.at[slot], j + 4, d).wait_send()
            rope_send(slot, j + 4, d).wait_send()
    own_q_cross.wait_send()
    for i in range(1, 4):
        q_send(i).wait_send()
        q_cross(i).wait_send()
    for i in range(1, 8):
        hv_send(i).wait_send()
        st_send(i).wait_send()
    for x in range(4):
        core_send(a_buf, a_rx, acs, acr, x).wait_send()
        core_send(m_buf, m_rx, mcs, mcr, x).wait_send()
        ag_cross(x).wait_send()
    for i in range(1, 16):
        scatter_send(a_sum, a_in, ars_s, ars_r, i % 4, i // 4).wait_send()
        scatter_send(m_sum, m_in, mrs_s, mrs_r, i % 4, i // 4).wait_send()
        ag_send(i % 4, i // 4).wait_send()


def on_device(
    hidden,
    queries,
    new_latents,
    suffix_cache,
    suffix_lengths,
    prompt_latents,
    value_up,
    out_proj,
    rms_gain,
    gate_ids,
    gate_weights,
    w_gate,
    w_up,
    w_down,
):
    any_spec = pl.BlockSpec(memory_space=pl.ANY)
    vmem = pl.BlockSpec(memory_space=pltpu.VMEM)
    smem = pl.BlockSpec(memory_space=pltpu.SMEM)
    sem = pltpu.SemaphoreType.DMA
    out = jax.ShapeDtypeStruct((8, 1792), BF)
    block = (16, HALF)
    scratch = [
        pltpu.VMEM((8, 256, LATK), BF),
        pltpu.VMEM((4, LATK, GROUP), BF),
        pltpu.VMEM((1024, LATK), BF),
        pltpu.VMEM((16, KC, LAT), BF),
        pltpu.VMEM((16, ROPE, KC), BF),
        pltpu.VMEM((2, LAT, GROUP), BF),
        pltpu.VMEM((LAT, GROUP), BF),
        pltpu.VMEM((1024, LATK), BF),
        pltpu.VMEM((128, LATK), BF),
        pltpu.VMEM((4, LAT, GROUP), F32),
        pltpu.VMEM((4, 1, GROUP), F32),
        pltpu.VMEM((4, 1, GROUP), F32),
        pltpu.VMEM((32, LAT, 128), BF),
        pltpu.VMEM((512, D), BF),
        pltpu.VMEM((D, 256), BF),
        pltpu.VMEM((D, 256), BF),
        pltpu.VMEM((256, D), BF),
        pltpu.VMEM((32, 4, 16, LAT), BF),
        pltpu.VMEM((32, 4, 16, 128), F32),
        pltpu.VMEM((8, 16, 2048), BF),
        pltpu.VMEM((8, 16, 2048), BF),
        pltpu.VMEM((8, 2, 2048), F32),
        pltpu.VMEM((2, 4, 4) + block, BF),
        pltpu.VMEM((4, 4) + block, BF),
        pltpu.VMEM((4, 4) + block, BF),
        pltpu.VMEM((16,) + block, BF),
        pltpu.VMEM((2, 4, 4) + block, BF),
        pltpu.VMEM((2, 4, 4) + block, BF),
        pltpu.VMEM((4, 4) + block, BF),
        pltpu.VMEM((4, 4) + block, BF),
        pltpu.VMEM((16,) + block, BF),
    ] + [sem((n,)) for n in (8, 12, 12, 12, 12, 4, 4, 4, 4, 8, 8, 8, 8, 4, 4, 16, 16, 16, 16, 4, 4, 4, 4, 16, 16)]
    attended, layer = pl.pallas_call(
        kernel,
        out_shape=(out, out),
        in_specs=[smem] + [vmem] * 5 + [any_spec] * 8,
        out_specs=(vmem, vmem),
        scratch_shapes=scratch,
        compiler_params=pltpu.CompilerParams(
            collective_id=0, has_side_effects=True, vmem_limit_bytes=62 * 2**20
        ),
    )(
        suffix_lengths,
        hidden,
        new_latents,
        rms_gain.reshape(8, 1, HALF),
        gate_ids,
        gate_weights,
        queries.reshape(256, LATK),
        prompt_latents,
        suffix_cache.reshape(1024, LATK),
        value_up,
        out_proj.reshape(512, D),
        w_gate[0],
        w_up[0],
        w_down[0],
    )
    return attended, layer


def solution(mesh):
    placed = (
        P(("prompt", "resp"), "expert"),
        P(("prompt", "resp"), "expert", None),
        P(("prompt", "resp"), None),
        P(("prompt", "resp"), None, None),
        P(("prompt", "resp")),
        P(("prompt", "resp", "expert"), None),
        P("expert", None, None),
        P("expert", "resp", None),
        P(),
        P("prompt", None),
        P("prompt", None),
        P("expert", None, "resp"),
        P("expert", None, "resp"),
        P("expert", "resp", None),
    )
    return jax.shard_map(
        on_device,
        mesh=mesh,
        in_specs=placed,
        out_specs=(P(("prompt", "resp"), "expert"), P(("prompt", "resp"), "expert")),
        check_vma=False,
    )
```

```python
import jax
import jax.numpy as jnp
from jax import lax
from jax.experimental import pallas as pl
from jax.experimental.pallas import tpu as pltpu
from jax.sharding import PartitionSpec as P

MESH = pl.DeviceIdType.MESH
BF = jnp.bfloat16
F32 = jnp.float32
LAT, ROPE, LATK = 512, 64, 576
SCALE2 = (128 + 64) ** -0.5 * 1.4426950408889634
FLOOR = -0.5e30
DEAD = -1e30
D = 7168
HALF = 896
KC = 256
GROUP = 512


def iota(shape, dim):
    return lax.broadcasted_iota(jnp.int32, shape, dim)


def dot(a, b):
    return jnp.dot(a, b, preferred_element_type=F32)


def kernel(
    slen,
    hid,
    newl,
    gain,
    gids,
    gwts,
    q_in,
    k_in,
    suf_in,
    vup_in,
    wo_in,
    wg_in,
    wu_in,
    wd_in,
    out_ref,
    q_own,
    q_all,
    place,
    qt,
    kt_own,
    kt_all,
    k_own,
    k_row,
    suf,
    nl,
    acc,
    mx,
    sm,
    vup,
    wo,
    wg,
    wu,
    wd,
    ctx,
    hv,
    hv_tx,
    hv_rx,
    st_rx,
    a_buf,
    a_rx,
    a_sum,
    a_in,
    ag,
    m_buf,
    m_rx,
    m_sum,
    m_in,
    ld,
    kss,
    krs,
    qss,
    qrs,
    qcs,
    qcr,
    near,
    far,
    hss,
    hrs,
    tss,
    trs,
    acs,
    acr,
    ars_s,
    ars_r,
    ags_s,
    ags_r,
    agc_s,
    agc_r,
    mcs,
    mcr,
    mrs_s,
    mrs_r,
):
    e = lax.axis_index("expert")
    r = lax.axis_index("resp")
    c = lax.rem(r, 2)
    z = r // 2
    right, left = lax.rem(e + 1, 4), lax.rem(e + 3, 4)
    twin = {"resp": z * 2 + 1 - c}

    def remote(src, dst, ssem, rsem, dev):
        return pltpu.make_async_remote_copy(
            src_ref=src, dst_ref=dst, send_sem=ssem, recv_sem=rsem, device_id=dev, device_id_type=MESH
        )

    def same_core(de, dz):
        return {"expert": lax.rem(e + de, 4), "resp": lax.rem(z + dz, 4) * 2 + c}

    loads = [
        pltpu.make_async_copy(q_in, q_own, ld.at[0]),
        pltpu.make_async_copy(k_in, kt_own, ld.at[1]),
        pltpu.make_async_copy(suf_in, suf, ld.at[2]),
        pltpu.make_async_copy(vup_in, vup, ld.at[3]),
        pltpu.make_async_copy(wo_in, wo, ld.at[4]),
        pltpu.make_async_copy(wg_in, wg, ld.at[5]),
        pltpu.make_async_copy(wu_in, wu, ld.at[6]),
        pltpu.make_async_copy(wd_in, wd, ld.at[7]),
    ]
    for x in loads[:3]:
        x.start()

    neighbours = [same_core(1, 0), same_core(3, 0), same_core(0, 1), same_core(0, 3), twin]
    bar = pltpu.get_barrier_semaphore()
    for x in neighbours:
        pl.semaphore_signal(bar, inc=1, device_id=x, device_id_type=MESH)
    loads[0].wait()
    q_all[r] = q_own[...].T
    pl.semaphore_wait(bar, 5)

    def k_send(src, j, d):
        dev = {"expert": right if d == 0 else left}
        return remote(src, kt_all.at[2 * j + d], kss.at[2 * j + d], krs.at[2 * j + d], dev)

    def own_chunk(j, d):
        return k_in.at[:, pl.ds(KC * (j if d == 0 else 3 - j), KC)]

    k_own_sends = [k_send(own_chunk(j, d), j, d) for j in range(4) for d in range(2)]

    def q_block(dz):
        return q_all.at[lax.rem(z + dz, 4) * 2 + c]

    half_rows = (pl.ds(0, LATK // 2), pl.ds(LATK // 2, LATK // 2))

    def q_send(i):
        if i < 2:
            part = q_block(0)
        else:
            part = q_block(3 if i == 2 else 1).at[half_rows[i - 2]]
        return remote(part, part, qss.at[i], qrs.at[i], same_core(0, 1 if i % 2 == 0 else 3))

    def q_come(i):
        if i < 2:
            part = q_block(3 if i == 0 else 1)
        else:
            part = q_block(2).at[half_rows[i - 2]]
        return remote(part, part, qss.at[i], qrs.at[i], same_core(0, 1 if i % 2 == 0 else 3))

    def q_cross(i):
        if i < 3:
            part = q_block((0, 3, 1)[i])
        else:
            part = q_block(2).at[half_rows[i - 3]]
        return remote(part, part, qcs.at[i], qcr.at[i], twin)

    def q_cross_come(i):
        if i < 3:
            part = q_all.at[lax.rem(z + (0, 3, 1)[i], 4) * 2 + 1 - c]
        else:
            part = q_all.at[lax.rem(z + 2, 4) * 2 + 1 - c].at[half_rows[i - 3]]
        return remote(part, part, qcs.at[i], qcr.at[i], twin)

    for x in k_own_sends[:2]:
        x.start()
    q_send(0).start()
    q_send(1).start()
    q_cross(0).start()
    for x in k_own_sends[2:]:
        x.start()
    for x in neighbours:
        pl.semaphore_signal(near, inc=1, device_id=x, device_id_type=MESH)

    mx[...] = jnp.full_like(mx, FLOOR)
    sm[...] = jnp.zeros_like(sm)
    acc[...] = jnp.zeros_like(acc)
    nl[...] = jnp.zeros_like(nl)
    nl[0:8, :] = newl[...]

    loads[1].wait()
    k_own[...] = kt_own[...].T

    def soft(s, g, vt):
        old = mx[g]
        new = jnp.maximum(old, jnp.max(s, axis=0, keepdims=True))
        mx[g] = new
        p = jnp.exp2((s - new) * SCALE2)
        shrink = jnp.exp2((old - new) * SCALE2)
        sm[g] = sm[g] * shrink + jnp.sum(p, axis=0, keepdims=True)
        acc[g] = acc[g] * shrink + dot(vt, p.astype(BF))

    row, col = iota((GROUP, GROUP), 0), iota((GROUP, GROUP), 1)
    want = ((col // 8) % 2) * 256 + (col % 8) * 32 + col // 16
    place[...] = jnp.where(row == want, 1.0, 0.0).astype(BF)

    def make_qt(g):
        block = jnp.concatenate([q_all[2 * g], q_all[2 * g + 1]], axis=1)
        qt[g] = dot(block, place[...]).astype(BF)

    def own_keys(g):
        s0 = dot(k_own[0:GROUP, :], qt[g])
        s1 = dot(k_own[GROUP : 2 * GROUP, :], qt[g])
        soft(s0, g, kt_own[0:LAT, 0:GROUP])
        soft(s1, g, kt_own[0:LAT, GROUP : 2 * GROUP])

    q_cross_come(0).wait_recv()
    make_qt(z)
    loads[2].wait()
    for x in loads[3:]:
        x.start()
    tok = iota((1, GROUP), 1) % 16
    mine = (tok // 8) == c
    for b in range(2):
        s = dot(suf[b].T, qt[z])
        live = (iota((GROUP, GROUP), 0) < slen[b]) & mine & ((tok % 8) // 4 == b)
        soft(jnp.where(live, s, DEAD), z, suf[b, 0:LAT, :])
    s = dot(nl[...], qt[z])
    key = iota((128, GROUP), 0)
    live = (key < 8) & mine & ((tok % 8) // 4 == key // 4) & (key % 4 <= tok % 4)
    soft(jnp.where(live, s, DEAD), z, nl[:, :LAT].T)
    own_keys(z)

    for i in range(2):
        q_come(i).wait_recv()
        q_cross(i + 1).start()
        q_send(i + 2).start()
    for i in range(2):
        g = lax.rem(z + (3, 1)[i], 4)
        q_cross_come(i + 1).wait_recv()
        make_qt(g)
        own_keys(g)
    for i in range(2):
        q_come(i + 2).wait_recv()
        q_cross(i + 3).start()
    for j in range(2):
        for d in range(2):
            k_send(kt_all.at[2 * j + d], j, d).wait_recv()
            k_send(kt_all.at[2 * j + d], j + 4, d).start()
    for i in range(2):
        q_cross_come(i + 3).wait_recv()
    make_qt(lax.rem(z + 2, 4))
    own_keys(lax.rem(z + 2, 4))
    pl.semaphore_wait(near, 5)
    for x in (same_core(2, 0), same_core(0, 2)):
        pl.semaphore_signal(far, inc=1, device_id=x, device_id_type=MESH)

    def arrive(j):
        for d in range(2):
            k_send(kt_all.at[2 * j + d], j, d).wait_recv()

    def pair(j):
        k_row[0:KC] = kt_all[2 * j].T
        k_row[KC : 2 * KC] = kt_all[2 * j + 1].T
        vt = jnp.concatenate([kt_all[2 * j, 0:LAT, :], kt_all[2 * j + 1, 0:LAT, :]], axis=1)

        s = dot(k_row[...], qt[0])
        for g in range(4):
            nxt = dot(k_row[...], qt[g + 1]) if g < 3 else None
            soft(s, g, vt)
            s = nxt

    def pair_last(j, carry):
        arrive(j)
        pair(j)
        return carry

    pair(0)
    pair(1)
    lax.fori_loop(2, 6, pair_last, 0)
    pl.semaphore_wait(far, 2)

    for g in range(4):
        part = (acc[g] * (1.0 / sm[g])).astype(BF)
        ctx[:, g] = part.T.reshape(32, 16, LAT)
    loads[3].wait()

    def project(h, carry):
        hv[h] = dot(ctx[h].reshape(64, LAT), vup[h]).reshape(4, 16, 128)
        return carry

    def hv_send(i, n):
        to = lax.rem(r + i, 8)
        return remote(hv_tx.at[n, to], hv_rx.at[n, i], hss.at[n, i], hrs.at[n, i], {"resp": to})

    def st_send(i):
        to = lax.rem(r + i, 8)
        return remote(st_rx.at[0], st_rx.at[i], tss.at[i], trs.at[i], {"resp": to})

    for g in range(4):
        for n in range(2):
            lanes = pl.ds(1024 * n + 256 * g, 256)
            st_rx[0, 0:1, lanes] = mx[g][:, 256 * n : 256 * n + 256]
            st_rx[0, 1:2, lanes] = sm[g][:, 256 * n : 256 * n + 256]
    for i in (4, 3, 5, 2, 6, 1, 7):
        st_send(i).start()
    for n in range(2):
        lax.fori_loop(16 * n, 16 * n + 16, project, 0, unroll=4)
        for g in range(4):
            for hb in range(2):
                first = 16 * n + 8 * hb
                block = hv[first : first + 8, g].reshape(128, 128).T.astype(BF)
                hv_tx[n, :, :, 256 * g + 128 * hb : 256 * g + 128 * hb + 128] = block.reshape(8, 16, 128)
        for i in (4, 3, 5, 2, 6, 1, 7):
            hv_send(i, n).start()

    for i in range(1, 8):
        st_send(i).wait_recv()
    top = st_rx[0, 0:1, :]
    for i in range(1, 8):
        top = jnp.maximum(top, st_rx[i, 0:1, :])
    weights = []
    total = None
    for i in range(8):
        w = st_rx[i, 1:2, :] * jnp.exp2((st_rx[i, 0:1, :] - top) * SCALE2)
        weights.append(w)
        total = w if total is None else total + w
    inv = 1.0 / total
    weights = [w * inv for w in weights]
    halves = []
    for n in range(2):
        lanes = slice(1024 * n, 1024 * n + 1024)
        y = hv_tx[n, r].astype(F32) * weights[0][:, lanes]
        for i in (4, 3, 5, 2, 6, 1, 7):
            hv_send(i, n).wait_recv()
            y = y + hv_rx[n, i].astype(F32) * weights[i][:, lanes]
        halves.append(y.astype(BF))

    col, row = iota((GROUP, 64), 1), iota((GROUP, 64), 0)
    want = ((row % 16) // 8) * 32 + (row // 128) * 8 + row % 8
    gather = jnp.where(col == want, 1.0, 0.0).astype(BF)
    keep = (iota((128, GROUP), 0) // 16) == ((iota((128, GROUP), 1) % 128) // 16)
    lhs = []
    for hb in range(4):
        piece = jnp.concatenate(
            [halves[hb // 2][:, 256 * g + 128 * (hb % 2) : 256 * g + 128 * (hb % 2) + 128] for g in range(4)],
            axis=1,
        )
        piece = jnp.concatenate([piece] * 8, axis=0)
        lhs.append(dot(jnp.where(keep, piece, jnp.zeros_like(piece)), gather))
    lhs = jnp.concatenate(lhs, axis=0).T.astype(BF)

    def core_send(buf, rx, ssem, rsem, x):
        return remote(buf.at[1 - c, x], rx.at[x], ssem.at[x], rsem.at[x], twin)

    def scatter_send(total_buf, landing, ssem, rsem, de, dz):
        src = total_buf.at[lax.rem(e + de, 4), lax.rem(z + dz, 4)]
        i = dz * 4 + de
        return remote(src, landing.at[i], ssem.at[i], rsem.at[i], same_core(de, dz))

    def fill(buf, x, tile):
        for cc in range(2):
            for g in range(4):
                rows = tile[32 * cc + 8 * g : 32 * cc + 8 * g + 8, :]
                buf[cc, x, g] = jnp.concatenate([rows[:, :HALF], rows[:, HALF:]], axis=0).astype(BF)

    def reduce_scatter(tile, buf, rx, total_buf, landing, cs, cr, ss, sr):
        def pass_on(de):
            x = lax.rem(e + de, 4)
            core_send(buf, rx, cs, cr, x).wait_recv()
            total_buf[x] = (buf[c, x].astype(F32) + rx[x].astype(F32)).astype(BF)
            for dz in (2, 1, 3, 0):
                if de or dz:
                    scatter_send(total_buf, landing, ss, sr, de, dz).start()

        last = None
        for de in (2, 1, 3, 0):
            x = lax.rem(e + de, 4)
            fill(buf, x, tile(x))
            core_send(buf, rx, cs, cr, x).start()
            if last is not None:
                pass_on(last)
            last = de
        pass_on(last)
        out = total_buf[e, z].astype(F32)
        for de in (2, 1, 3, 0):
            for dz in (2, 1, 3, 0):
                if de or dz:
                    scatter_send(total_buf, landing, ss, sr, de, dz).wait_recv()
                    out = out + landing[dz * 4 + de].astype(F32)
        return out

    def columns(x):
        return pl.ds(pl.multiple_of(x * 1792, 128), 1792)

    loads[4].wait()
    attended = reduce_scatter(
        lambda x: dot(lhs, wo[:, columns(x)]), a_buf, a_rx, a_sum, a_in, acs, acr, ars_s, ars_r
    ).astype(BF)
    hidden = jnp.concatenate([hid[:, :HALF], hid[:, HALF:]], axis=0)
    resid = (hidden.astype(F32) + attended.astype(F32)).astype(BF)
    ag[c, e, z] = resid
    out_ref[0] = jnp.concatenate([attended[0:8], attended[8:16]], axis=1)

    def ag_send(de, dz):
        i = dz * 4 + de
        return remote(ag.at[c, e, z], ag.at[c, e, z], ags_s.at[i], ags_r.at[i], same_core(de, dz))

    def ag_cross(x):
        return remote(ag.at[c, x], ag.at[c, x], agc_s.at[x], agc_r.at[x], twin)

    for de in (0, 1, 3, 2):
        for dz in range(4):
            if de or dz:
                ag_send(de, dz).start()

    loads[5].wait()
    loads[6].wait()
    squares = jnp.zeros((64, 1), F32)
    gate = jnp.zeros((64, 256), F32)
    up = jnp.zeros((64, 256), F32)
    def features(de, squares, gate, up):
        x = lax.rem(e + 4 - de, 4)
        ag_cross(x).wait_recv()
        wide = ag[:, x].astype(F32)
        for half in range(2):
            part = wide[:, :, 8 * half : 8 * half + 8, :].reshape(64, HALF)
            squares = squares + jnp.sum(part * part, axis=1, keepdims=True)
            scaled = (part * gain[2 * x + half]).astype(BF)
            rows = pl.ds(pl.multiple_of(x * 1792 + half * HALF, HALF), HALF)
            gate = gate + dot(scaled, wg[rows, :])
            up = up + dot(scaled, wu[rows, :])
        return squares, gate, up

    last = None
    for de in (0, 1, 3, 2):
        for dz in range(4):
            if de or dz:
                ag_send(de, dz).wait_recv()
        ag_cross(lax.rem(e + 4 - de, 4)).start()
        if last is not None:
            squares, gate, up = features(last, squares, gate, up)
        last = de
    squares, gate, up = features(last, squares, gate, up)
    norm = lax.rsqrt(squares * (1.0 / D) + 1e-6)
    gate = gate * norm
    up = up * norm
    act = (gate / (1.0 + jnp.exp(-gate)) * up).astype(BF)

    picked = jnp.where(gids[...] == e, gwts[...], 0.0)
    share = 2.5 * jnp.sum(picked, axis=0, keepdims=True) / jnp.sum(gwts[...], axis=0, keepdims=True)
    row, tok = iota((64, 64), 0), iota((64, 64), 1)
    here = tok == ((row // 8) % 4) * 16 + (row // 32) * 8 + row % 8
    share = jnp.sum(jnp.where(here, share, 0.0), axis=1, keepdims=True)
    loads[7].wait()
    moe = reduce_scatter(
        lambda x: dot(act, wd[:, columns(x)]) * share, m_buf, m_rx, m_sum, m_in, mcs, mcr, mrs_s, mrs_r
    )
    out = (resid.astype(F32) + moe).astype(BF)
    out_ref[1] = jnp.concatenate([out[0:8], out[8:16]], axis=1)

    for x in k_own_sends:
        x.wait_send()
    for j in range(2):
        for d in range(2):
            k_send(kt_all.at[2 * j + d], j + 4, d).wait_send()
    for i in range(4):
        q_send(i).wait_send()
    for i in range(5):
        q_cross(i).wait_send()
    for i in range(1, 8):
        st_send(i).wait_send()
        for n in range(2):
            hv_send(i, n).wait_send()
    for x in range(4):
        core_send(a_buf, a_rx, acs, acr, x).wait_send()
        core_send(m_buf, m_rx, mcs, mcr, x).wait_send()
        ag_cross(x).wait_send()
    for i in range(1, 16):
        scatter_send(a_sum, a_in, ars_s, ars_r, i % 4, i // 4).wait_send()
        scatter_send(m_sum, m_in, mrs_s, mrs_r, i % 4, i // 4).wait_send()
        ag_send(i % 4, i // 4).wait_send()


def on_device(
    hidden,
    queries,
    new_latents,
    suffix_cache,
    suffix_lengths,
    prompt_latents,
    value_up,
    out_proj,
    rms_gain,
    gate_ids,
    gate_weights,
    w_gate,
    w_up,
    w_down,
):
    any_spec = pl.BlockSpec(memory_space=pl.ANY)
    vmem = pl.BlockSpec(memory_space=pltpu.VMEM)
    smem = pl.BlockSpec(memory_space=pltpu.SMEM)
    sem = pltpu.SemaphoreType.DMA
    out = jax.ShapeDtypeStruct((2, 8, 1792), BF)
    block = (16, HALF)
    scratch = [
        pltpu.VMEM((256, LATK), BF),
        pltpu.VMEM((8, LATK, 256), BF),
        pltpu.VMEM((GROUP, GROUP), BF),
        pltpu.VMEM((4, LATK, GROUP), BF),
        pltpu.VMEM((LATK, 1024), BF),
        pltpu.VMEM((12, LATK, KC), BF),
        pltpu.VMEM((1024, LATK), BF),
        pltpu.VMEM((GROUP, LATK), BF),
        pltpu.VMEM((2, LATK, GROUP), BF),
        pltpu.VMEM((128, LATK), BF),
        pltpu.VMEM((4, LAT, GROUP), F32),
        pltpu.VMEM((4, 1, GROUP), F32),
        pltpu.VMEM((4, 1, GROUP), F32),
        pltpu.VMEM((32, LAT, 128), BF),
        pltpu.VMEM((512, D), BF),
        pltpu.VMEM((D, 256), BF),
        pltpu.VMEM((D, 256), BF),
        pltpu.VMEM((256, D), BF),
        pltpu.VMEM((32, 4, 16, LAT), BF),
        pltpu.VMEM((32, 4, 16, 128), F32),
        pltpu.VMEM((2, 8, 16, 1024), BF),
        pltpu.VMEM((2, 8, 16, 1024), BF),
        pltpu.VMEM((8, 2, 2048), F32),
        pltpu.VMEM((2, 4, 4) + block, BF),
        pltpu.VMEM((4, 4) + block, BF),
        pltpu.VMEM((4, 4) + block, BF),
        pltpu.VMEM((16,) + block, BF),
        pltpu.VMEM((2, 4, 4) + block, BF),
        pltpu.VMEM((2, 4, 4) + block, BF),
        pltpu.VMEM((4, 4) + block, BF),
        pltpu.VMEM((4, 4) + block, BF),
        pltpu.VMEM((16,) + block, BF),
    ]
    scratch += [sem((n,)) for n in (8, 12, 12, 4, 4, 5, 5)]
    scratch += [pltpu.SemaphoreType.REGULAR, pltpu.SemaphoreType.REGULAR]
    scratch += [sem((2, 8)), sem((2, 8))]
    scratch += [sem((n,)) for n in (8, 8, 4, 4, 16, 16, 16, 16, 4, 4, 4, 4, 16, 16)]
    both = pl.pallas_call(
        kernel,
        out_shape=out,
        in_specs=[smem] + [vmem] * 5 + [any_spec] * 8,
        out_specs=vmem,
        scratch_shapes=scratch,
        compiler_params=pltpu.CompilerParams(
            collective_id=0, has_side_effects=True, vmem_limit_bytes=62 * 2**20
        ),
    )(
        suffix_lengths,
        hidden,
        new_latents,
        rms_gain.reshape(8, 1, HALF),
        gate_ids.T,
        gate_weights.T,
        queries.reshape(256, LATK),
        prompt_latents.T,
        jnp.swapaxes(suffix_cache, 1, 2),
        value_up,
        out_proj.reshape(512, D),
        w_gate[0],
        w_up[0],
        w_down[0],
    )
    return both[0], both[1]


def solution(mesh):
    placed = (
        P(("prompt", "resp"), "expert"),
        P(("prompt", "resp"), "expert", None),
        P(("prompt", "resp"), None),
        P(("prompt", "resp"), None, None),
        P(("prompt", "resp")),
        P(("prompt", "resp", "expert"), None),
        P("expert", None, None),
        P("expert", "resp", None),
        P(),
        P("prompt", None),
        P("prompt", None),
        P("expert", None, "resp"),
        P("expert", None, "resp"),
        P("expert", "resp", None),
    )
    return jax.shard_map(
        on_device,
        mesh=mesh,
        in_specs=placed,
        out_specs=(P(("prompt", "resp"), "expert"), P(("prompt", "resp"), "expert")),
        check_vma=False,
    )
```

```python
import jax
import jax.numpy as jnp
from jax import lax
from jax.experimental import pallas as pl
from jax.experimental.pallas import tpu as pltpu
from jax.sharding import PartitionSpec as P

MESH = pl.DeviceIdType.MESH
BF = jnp.bfloat16
F32 = jnp.float32
LAT, ROPE, LATK = 512, 64, 576
SCALE2 = (128 + 64) ** -0.5 * 1.4426950408889634
FLOOR = -0.5e30
DEAD = -1e30
D = 7168
HALF = 896
KC = 256
GROUP = 512


def iota(shape, dim):
    return lax.broadcasted_iota(jnp.int32, shape, dim)


def dot(a, b):
    return jnp.dot(a, b, preferred_element_type=F32)


def kernel(
    slen,
    hid,
    newl,
    gain,
    gids,
    gwts,
    q_in,
    k_in,
    suf_in,
    vup_in,
    wo_in,
    wg_in,
    wu_in,
    wd_in,
    out_ref,
    q_own,
    q_all,
    place,
    qt,
    kt_own,
    kt_all,
    k_own,
    k_row,
    suf,
    nl,
    acc,
    mx,
    sm,
    vup,
    wo,
    wg,
    wu,
    wd,
    ctx,
    hv,
    hv_tx,
    hv_tw,
    st_own,
    st_tw,
    z_tx,
    z_rx,
    st_z,
    a_buf,
    a_rx,
    a_sum,
    a_in,
    ag,
    m_buf,
    m_rx,
    m_sum,
    m_in,
    ld,
    kss,
    krs,
    qss,
    qrs,
    qcs,
    qcr,
    near,
    far,
    tws,
    twr,
    tss,
    tsr,
    zss,
    zrs,
    zts,
    ztr,
    acs,
    acr,
    ars_s,
    ars_r,
    ags_s,
    ags_r,
    agc_s,
    agc_r,
    mcs,
    mcr,
    mrs_s,
    mrs_r,
):
    e = lax.axis_index("expert")
    r = lax.axis_index("resp")
    c = lax.rem(r, 2)
    z = r // 2
    right, left = lax.rem(e + 1, 4), lax.rem(e + 3, 4)
    twin = {"resp": z * 2 + 1 - c}

    def remote(src, dst, ssem, rsem, dev):
        return pltpu.make_async_remote_copy(
            src_ref=src, dst_ref=dst, send_sem=ssem, recv_sem=rsem, device_id=dev, device_id_type=MESH
        )

    def same_core(de, dz):
        return {"expert": lax.rem(e + de, 4), "resp": lax.rem(z + dz, 4) * 2 + c}

    loads = [
        pltpu.make_async_copy(q_in, q_own, ld.at[0]),
        pltpu.make_async_copy(k_in, kt_own, ld.at[1]),
        pltpu.make_async_copy(suf_in, suf, ld.at[2]),
        pltpu.make_async_copy(vup_in, vup, ld.at[3]),
        pltpu.make_async_copy(wo_in, wo, ld.at[4]),
        pltpu.make_async_copy(wg_in, wg, ld.at[5]),
        pltpu.make_async_copy(wu_in, wu, ld.at[6]),
        pltpu.make_async_copy(wd_in, wd, ld.at[7]),
    ]
    for x in loads[:3]:
        x.start()

    neighbours = [same_core(1, 0), same_core(3, 0), same_core(0, 1), same_core(0, 3), twin]
    bar = pltpu.get_barrier_semaphore()
    for x in neighbours:
        pl.semaphore_signal(bar, inc=1, device_id=x, device_id_type=MESH)
    loads[0].wait()
    q_all[r] = q_own[...].T
    pl.semaphore_wait(bar, 5)

    def k_send(src, j, d):
        dev = {"expert": right if d == 0 else left}
        return remote(src, kt_all.at[2 * j + d], kss.at[2 * j + d], krs.at[2 * j + d], dev)

    def own_chunk(j, d):
        return k_in.at[:, pl.ds(KC * (j if d == 0 else 3 - j), KC)]

    def k_forward(j, d):
        dev = {"expert": right if d == 0 else left}
        if j == 0:
            return [k_send(kt_all.at[d], 4, d)]
        sems = (10 + d, 12 + d)
        return [
            remote(
                kt_all.at[2 + d, :, pl.ds(128 * i, 128)],
                kt_all.at[10 + d, :, pl.ds(128 * i, 128)],
                kss.at[sems[i]],
                krs.at[sems[i]],
                dev,
            )
            for i in range(2)
        ]

    k_own_sends = [k_send(own_chunk(j, d), j, d) for j in range(4) for d in range(2)]

    def q_block(dz):
        return q_all.at[lax.rem(z + dz, 4) * 2 + c]

    half_rows = (pl.ds(0, LATK // 2), pl.ds(LATK // 2, LATK // 2))

    def q_send(i):
        if i < 2:
            part = q_block(0)
        else:
            part = q_block(3 if i == 2 else 1).at[half_rows[i - 2]]
        return remote(part, part, qss.at[i], qrs.at[i], same_core(0, 1 if i % 2 == 0 else 3))

    def q_come(i):
        if i < 2:
            part = q_block(3 if i == 0 else 1)
        else:
            part = q_block(2).at[half_rows[i - 2]]
        return remote(part, part, qss.at[i], qrs.at[i], same_core(0, 1 if i % 2 == 0 else 3))

    def q_cross(i):
        if i < 3:
            part = q_block((0, 3, 1)[i])
        else:
            part = q_block(2).at[half_rows[i - 3]]
        return remote(part, part, qcs.at[i], qcr.at[i], twin)

    def q_cross_come(i):
        if i < 3:
            part = q_all.at[lax.rem(z + (0, 3, 1)[i], 4) * 2 + 1 - c]
        else:
            part = q_all.at[lax.rem(z + 2, 4) * 2 + 1 - c].at[half_rows[i - 3]]
        return remote(part, part, qcs.at[i], qcr.at[i], twin)

    for x in k_own_sends[:2]:
        x.start()
    q_send(0).start()
    q_send(1).start()
    q_cross(0).start()
    for x in k_own_sends[2:]:
        x.start()
    for x in neighbours:
        pl.semaphore_signal(near, inc=1, device_id=x, device_id_type=MESH)

    mx[...] = jnp.full_like(mx, FLOOR)
    sm[...] = jnp.zeros_like(sm)
    acc[...] = jnp.zeros_like(acc)
    nl[...] = jnp.zeros_like(nl)
    nl[0:8, :] = newl[...]

    loads[1].wait()
    k_own[...] = kt_own[...].T

    def soft(s, g, vt):
        old = mx[g]
        new = jnp.maximum(old, jnp.max(s, axis=0, keepdims=True))
        mx[g] = new
        p = jnp.exp2((s - new) * SCALE2)
        shrink = jnp.exp2((old - new) * SCALE2)
        sm[g] = sm[g] * shrink + jnp.sum(p, axis=0, keepdims=True)
        acc[g] = acc[g] * shrink + dot(vt, p.astype(BF))

    row, col = iota((GROUP, GROUP), 0), iota((GROUP, GROUP), 1)
    want = ((col // 8) % 2) * 256 + (col % 8) * 32 + col // 16
    place[...] = jnp.where(row == want, 1.0, 0.0).astype(BF)

    def make_qt(g):
        block = jnp.concatenate([q_all[2 * g], q_all[2 * g + 1]], axis=1)
        qt[g] = dot(block, place[...]).astype(BF)

    def own_keys(g):
        s0 = dot(k_own[0:GROUP, :], qt[g])
        s1 = dot(k_own[GROUP : 2 * GROUP, :], qt[g])
        soft(s0, g, kt_own[0:LAT, 0:GROUP])
        soft(s1, g, kt_own[0:LAT, GROUP : 2 * GROUP])

    q_cross_come(0).wait_recv()
    make_qt(z)
    loads[2].wait()
    for x in loads[3:]:
        x.start()
    tok = iota((1, GROUP), 1) % 16
    mine = (tok // 8) == c
    for b in range(2):
        s = dot(suf[b].T, qt[z])
        live = (iota((GROUP, GROUP), 0) < slen[b]) & mine & ((tok % 8) // 4 == b)
        soft(jnp.where(live, s, DEAD), z, suf[b, 0:LAT, :])
    s = dot(nl[...], qt[z])
    key = iota((128, GROUP), 0)
    live = (key < 8) & mine & ((tok % 8) // 4 == key // 4) & (key % 4 <= tok % 4)
    soft(jnp.where(live, s, DEAD), z, nl[:, :LAT].T)
    own_keys(z)

    for i in range(2):
        q_come(i).wait_recv()
        q_cross(i + 1).start()
        q_send(i + 2).start()
    for i in range(2):
        g = lax.rem(z + (3, 1)[i], 4)
        q_cross_come(i + 1).wait_recv()
        make_qt(g)
        own_keys(g)
    for i in range(2):
        q_come(i + 2).wait_recv()
        q_cross(i + 3).start()
    for j in range(2):
        for d in range(2):
            k_send(kt_all.at[2 * j + d], j, d).wait_recv()
            for x in k_forward(j, d):
                x.start()
    for i in range(2):
        q_cross_come(i + 3).wait_recv()
    make_qt(lax.rem(z + 2, 4))
    own_keys(lax.rem(z + 2, 4))
    pl.semaphore_wait(near, 5)
    for x in (same_core(2, 0), same_core(0, 2)):
        pl.semaphore_signal(far, inc=1, device_id=x, device_id_type=MESH)

    def arrive(j):
        for d in range(2):
            k_send(kt_all.at[2 * j + d], j, d).wait_recv()

    def keys_of(pieces):
        at = 0
        for slot, first, width in pieces:
            k_row[at : at + width] = kt_all[slot, :, first : first + width].T
            at += width
        return jnp.concatenate([kt_all[slot, 0:LAT, first : first + width] for slot, first, width in pieces], axis=1)

    def groups(count, vt):
        s = dot(k_row[0:count], qt[0])
        for g in range(4):
            nxt = dot(k_row[0:count], qt[g + 1]) if g < 3 else None
            soft(s, g, vt)
            s = nxt

    def pair(j):
        vt = keys_of([(2 * j, 0, KC), (2 * j + 1, 0, KC)])
        groups(GROUP, vt)

    def pair_last(j, carry):
        arrive(j)
        pair(j)
        return carry

    pair(0)
    pair(1)
    lax.fori_loop(2, 5, pair_last, 0)
    for d in range(2):
        k_forward(1, d)[0].wait_recv()
    groups(KC, keys_of([(10, 0, 128), (11, 0, 128)]))
    pl.semaphore_wait(far, 2)
    loads[3].wait()
    for d in range(2):
        k_forward(1, d)[1].wait_recv()
    vt = keys_of([(10, 128, 128), (11, 128, 128)])

    def lanes_of(ref, q):
        return jnp.concatenate([ref[g, :, 128 * q : 128 * q + 128] for g in range(4)], axis=1)

    def last_scores(q):
        return dot(k_row[0:KC], lanes_of(qt, q))

    def finish(q, s):
        old = lanes_of(mx, q)
        new = jnp.maximum(old, jnp.max(s, axis=0, keepdims=True))
        p = jnp.exp2((s - new) * SCALE2)
        shrink = jnp.exp2((old - new) * SCALE2)
        total = lanes_of(sm, q) * shrink + jnp.sum(p, axis=0, keepdims=True)
        part = (lanes_of(acc, q) * shrink + dot(vt, p.astype(BF))) * (1.0 / total)
        st_own[q, 0:1, :] = new
        st_own[q, 1:2, :] = total
        ctx[q] = part.astype(BF).T.reshape(4, 8, 16, LAT)
        for h in range(8):
            hv[8 * q + h] = dot(ctx[q, :, h].reshape(64, LAT), vup[8 * q + h]).reshape(4, 16, 128)
        for g in range(4):
            block = hv[8 * q : 8 * q + 8, g].reshape(128, 128).T.astype(BF).reshape(4, 2, 16, 128)
            for cc in range(2):
                hv_tx[q, cc, :, :, 128 * g : 128 * g + 128] = block[:, cc]

    def twin_sends(q):
        return [
            remote(hv_tx.at[q, 1 - c], hv_tw.at[q], tws.at[q], twr.at[q], twin),
            remote(st_own.at[q], st_tw.at[q], tss.at[q], tsr.at[q], twin),
        ]

    def z_sends(q, dz):
        to = lax.rem(z + dz, 4)
        dev = same_core(0, dz)
        return [
            remote(z_tx.at[q, to], z_rx.at[q, dz], zss.at[q, dz], zrs.at[q, dz], dev),
            remote(st_z.at[q, 0], st_z.at[q, dz], zts.at[q, dz], ztr.at[q, dz], dev),
        ]

    def weight(st, top):
        return st[1:2, :] * jnp.exp2((st[0:1, :] - top) * SCALE2)

    def chip_sum(q):
        for x in twin_sends(q):
            x.wait_recv()
        top = jnp.maximum(st_own[q, 0:1, :], st_tw[q, 0:1, :])
        w1, w2 = weight(st_own[q], top), weight(st_tw[q], top)
        inv = 1.0 / (w1 + w2)
        mine = hv_tx[q, c].astype(F32) * (w1 * inv) + hv_tw[q].astype(F32) * (w2 * inv)
        z_tx[q] = mine.astype(BF)
        st_z[q, 0, 0:1, :] = top
        st_z[q, 0, 1:2, :] = w1 + w2
        for dz in (2, 1, 3):
            for x in z_sends(q, dz):
                x.start()

    def plane_sum(q):
        for dz in (2, 1, 3):
            for x in z_sends(q, dz):
                x.wait_recv()
        top = st_z[q, 0, 0:1, :]
        for dz in range(1, 4):
            top = jnp.maximum(top, st_z[q, dz, 0:1, :])
        w = [weight(st_z[q, dz], top) for dz in range(4)]
        y = z_tx[q, z].astype(F32) * w[0]
        for dz in range(1, 4):
            y = y + z_rx[q, dz].astype(F32) * w[dz]
        return (y * (1.0 / (w[0] + w[1] + w[2] + w[3]))).astype(BF)

    s = last_scores(0)
    for q in range(4):
        nxt = last_scores(q + 1) if q < 3 else None
        finish(q, s)
        for x in twin_sends(q):
            x.start()
        if q > 0:
            chip_sum(q - 1)
        s = nxt
    chip_sum(3)

    col, row = iota((GROUP, 64), 1), iota((GROUP, 64), 0)
    want = ((row % 16) // 8) * 32 + (row // 128) * 8 + row % 8
    gather = jnp.where(col == want, 1.0, 0.0).astype(BF)
    keep = (iota((128, GROUP), 0) // 16) == ((iota((128, GROUP), 1) % 128) // 16)
    lhs = []
    for hb in range(4):
        piece = plane_sum(hb)
        piece = jnp.concatenate([piece] * 8, axis=0)
        lhs.append(dot(jnp.where(keep, piece, jnp.zeros_like(piece)), gather))
    lhs = jnp.concatenate(lhs, axis=0).T.astype(BF)

    def core_send(buf, rx, ssem, rsem, x):
        return remote(buf.at[1 - c, x], rx.at[x], ssem.at[x], rsem.at[x], twin)

    def scatter_send(total_buf, landing, ssem, rsem, de, dz):
        src = total_buf.at[lax.rem(e + de, 4), lax.rem(z + dz, 4)]
        i = dz * 4 + de
        return remote(src, landing.at[i], ssem.at[i], rsem.at[i], same_core(de, dz))

    def fill(buf, x, tile):
        for cc in range(2):
            for g in range(4):
                rows = tile[32 * cc + 8 * g : 32 * cc + 8 * g + 8, :]
                buf[cc, x, g] = jnp.concatenate([rows[:, :HALF], rows[:, HALF:]], axis=0).astype(BF)

    def reduce_scatter(tile, buf, rx, total_buf, landing, cs, cr, ss, sr):
        def pass_on(de):
            x = lax.rem(e + de, 4)
            core_send(buf, rx, cs, cr, x).wait_recv()
            total_buf[x] = (buf[c, x].astype(F32) + rx[x].astype(F32)).astype(BF)
            for dz in (2, 1, 3, 0):
                if de or dz:
                    scatter_send(total_buf, landing, ss, sr, de, dz).start()

        last = None
        for de in (2, 1, 3, 0):
            x = lax.rem(e + de, 4)
            fill(buf, x, tile(x))
            core_send(buf, rx, cs, cr, x).start()
            if last is not None:
                pass_on(last)
            last = de
        pass_on(last)
        out = total_buf[e, z].astype(F32)
        for de in (2, 1, 3, 0):
            for dz in (2, 1, 3, 0):
                if de or dz:
                    scatter_send(total_buf, landing, ss, sr, de, dz).wait_recv()
                    out = out + landing[dz * 4 + de].astype(F32)
        return out

    def columns(x):
        return pl.ds(pl.multiple_of(x * 1792, 128), 1792)

    loads[4].wait()
    attended = reduce_scatter(
        lambda x: dot(lhs, wo[:, columns(x)]), a_buf, a_rx, a_sum, a_in, acs, acr, ars_s, ars_r
    ).astype(BF)
    hidden = jnp.concatenate([hid[:, :HALF], hid[:, HALF:]], axis=0)
    resid = (hidden.astype(F32) + attended.astype(F32)).astype(BF)
    ag[c, e, z] = resid
    out_ref[0] = jnp.concatenate([attended[0:8], attended[8:16]], axis=1)

    def ag_send(de, dz):
        i = dz * 4 + de
        return remote(ag.at[c, e, z], ag.at[c, e, z], ags_s.at[i], ags_r.at[i], same_core(de, dz))

    def ag_cross(x):
        return remote(ag.at[c, x], ag.at[c, x], agc_s.at[x], agc_r.at[x], twin)

    for de in (0, 1, 3, 2):
        for dz in range(4):
            if de or dz:
                ag_send(de, dz).start()

    loads[5].wait()
    loads[6].wait()
    squares = jnp.zeros((64, 1), F32)
    gate = jnp.zeros((64, 256), F32)
    up = jnp.zeros((64, 256), F32)
    def features(de, squares, gate, up):
        x = lax.rem(e + 4 - de, 4)
        ag_cross(x).wait_recv()
        wide = ag[:, x].astype(F32)
        for half in range(2):
            part = wide[:, :, 8 * half : 8 * half + 8, :].reshape(64, HALF)
            squares = squares + jnp.sum(part * part, axis=1, keepdims=True)
            scaled = (part * gain[2 * x + half]).astype(BF)
            rows = pl.ds(pl.multiple_of(x * 1792 + half * HALF, HALF), HALF)
            gate = gate + dot(scaled, wg[rows, :])
            up = up + dot(scaled, wu[rows, :])
        return squares, gate, up

    last = None
    for de in (0, 1, 3, 2):
        for dz in range(4):
            if de or dz:
                ag_send(de, dz).wait_recv()
        ag_cross(lax.rem(e + 4 - de, 4)).start()
        if last is not None:
            squares, gate, up = features(last, squares, gate, up)
        last = de
    squares, gate, up = features(last, squares, gate, up)
    norm = lax.rsqrt(squares * (1.0 / D) + 1e-6)
    gate = gate * norm
    up = up * norm
    act = (gate / (1.0 + jnp.exp(-gate)) * up).astype(BF)

    picked = jnp.where(gids[...] == e, gwts[...], 0.0)
    share = 2.5 * jnp.sum(picked, axis=0, keepdims=True) / jnp.sum(gwts[...], axis=0, keepdims=True)
    row, tok = iota((64, 64), 0), iota((64, 64), 1)
    here = tok == ((row // 8) % 4) * 16 + (row // 32) * 8 + row % 8
    share = jnp.sum(jnp.where(here, share, 0.0), axis=1, keepdims=True)
    loads[7].wait()
    moe = reduce_scatter(
        lambda x: dot(act, wd[:, columns(x)]) * share, m_buf, m_rx, m_sum, m_in, mcs, mcr, mrs_s, mrs_r
    )
    out = (resid.astype(F32) + moe).astype(BF)
    out_ref[1] = jnp.concatenate([out[0:8], out[8:16]], axis=1)

    for x in k_own_sends:
        x.wait_send()
    for j in range(2):
        for d in range(2):
            for x in k_forward(j, d):
                x.wait_send()
    for i in range(4):
        q_send(i).wait_send()
    for i in range(5):
        q_cross(i).wait_send()
    for q in range(4):
        for x in twin_sends(q):
            x.wait_send()
        for dz in range(1, 4):
            for x in z_sends(q, dz):
                x.wait_send()
    for x in range(4):
        core_send(a_buf, a_rx, acs, acr, x).wait_send()
        core_send(m_buf, m_rx, mcs, mcr, x).wait_send()
        ag_cross(x).wait_send()
    for i in range(1, 16):
        scatter_send(a_sum, a_in, ars_s, ars_r, i % 4, i // 4).wait_send()
        scatter_send(m_sum, m_in, mrs_s, mrs_r, i % 4, i // 4).wait_send()
        ag_send(i % 4, i // 4).wait_send()


def on_device(
    hidden,
    queries,
    new_latents,
    suffix_cache,
    suffix_lengths,
    prompt_latents,
    value_up,
    out_proj,
    rms_gain,
    gate_ids,
    gate_weights,
    w_gate,
    w_up,
    w_down,
):
    any_spec = pl.BlockSpec(memory_space=pl.ANY)
    vmem = pl.BlockSpec(memory_space=pltpu.VMEM)
    smem = pl.BlockSpec(memory_space=pltpu.SMEM)
    sem = pltpu.SemaphoreType.DMA
    out = jax.ShapeDtypeStruct((2, 8, 1792), BF)
    block = (16, HALF)
    scratch = [
        pltpu.VMEM((256, LATK), BF),
        pltpu.VMEM((8, LATK, 256), BF),
        pltpu.VMEM((GROUP, GROUP), BF),
        pltpu.VMEM((4, LATK, GROUP), BF),
        pltpu.VMEM((LATK, 1024), BF),
        pltpu.VMEM((12, LATK, KC), BF),
        pltpu.VMEM((1024, LATK), BF),
        pltpu.VMEM((GROUP, LATK), BF),
        pltpu.VMEM((2, LATK, GROUP), BF),
        pltpu.VMEM((128, LATK), BF),
        pltpu.VMEM((4, LAT, GROUP), F32),
        pltpu.VMEM((4, 1, GROUP), F32),
        pltpu.VMEM((4, 1, GROUP), F32),
        pltpu.VMEM((32, LAT, 128), BF),
        pltpu.VMEM((512, D), BF),
        pltpu.VMEM((D, 256), BF),
        pltpu.VMEM((D, 256), BF),
        pltpu.VMEM((256, D), BF),
        pltpu.VMEM((4, 4, 8, 16, LAT), BF),
        pltpu.VMEM((32, 4, 16, 128), F32),
        pltpu.VMEM((4, 2, 4, 16, GROUP), BF),
        pltpu.VMEM((4, 4, 16, GROUP), BF),
        pltpu.VMEM((4, 2, GROUP), F32),
        pltpu.VMEM((4, 2, GROUP), F32),
        pltpu.VMEM((4, 4, 16, GROUP), BF),
        pltpu.VMEM((4, 4, 16, GROUP), BF),
        pltpu.VMEM((4, 4, 2, GROUP), F32),
        pltpu.VMEM((2, 4, 4) + block, BF),
        pltpu.VMEM((4, 4) + block, BF),
        pltpu.VMEM((4, 4) + block, BF),
        pltpu.VMEM((16,) + block, BF),
        pltpu.VMEM((2, 4, 4) + block, BF),
        pltpu.VMEM((2, 4, 4) + block, BF),
        pltpu.VMEM((4, 4) + block, BF),
        pltpu.VMEM((4, 4) + block, BF),
        pltpu.VMEM((16,) + block, BF),
    ]
    scratch += [sem((n,)) for n in (8, 14, 14, 4, 4, 5, 5)]
    scratch += [pltpu.SemaphoreType.REGULAR, pltpu.SemaphoreType.REGULAR]
    scratch += [sem((4,))] * 4 + [sem((4, 4))] * 4
    scratch += [sem((n,)) for n in (4, 4, 16, 16, 16, 16, 4, 4, 4, 4, 16, 16)]
    both = pl.pallas_call(
        kernel,
        out_shape=out,
        in_specs=[smem] + [vmem] * 5 + [any_spec] * 8,
        out_specs=vmem,
        scratch_shapes=scratch,
        compiler_params=pltpu.CompilerParams(
            collective_id=0, has_side_effects=True, vmem_limit_bytes=62 * 2**20
        ),
    )(
        suffix_lengths,
        hidden,
        new_latents,
        rms_gain.reshape(8, 1, HALF),
        gate_ids.T,
        gate_weights.T,
        queries.reshape(256, LATK),
        prompt_latents.T,
        jnp.swapaxes(suffix_cache, 1, 2),
        value_up,
        out_proj.reshape(512, D),
        w_gate[0],
        w_up[0],
        w_down[0],
    )
    return both[0], both[1]


def solution(mesh):
    placed = (
        P(("prompt", "resp"), "expert"),
        P(("prompt", "resp"), "expert", None),
        P(("prompt", "resp"), None),
        P(("prompt", "resp"), None, None),
        P(("prompt", "resp")),
        P(("prompt", "resp", "expert"), None),
        P("expert", None, None),
        P("expert", "resp", None),
        P(),
        P("prompt", None),
        P("prompt", None),
        P("expert", None, "resp"),
        P("expert", None, "resp"),
        P("expert", "resp", None),
    )
    return jax.shard_map(
        on_device,
        mesh=mesh,
        in_specs=placed,
        out_specs=(P(("prompt", "resp"), "expert"), P(("prompt", "resp"), "expert")),
        check_vma=False,
    )
```

```python
import jax
import jax.numpy as jnp
from jax import lax
from jax.experimental import pallas as pl
from jax.experimental.pallas import tpu as pltpu
from jax.sharding import PartitionSpec as P

MESH = pl.DeviceIdType.MESH
BF = jnp.bfloat16
F32 = jnp.float32
LAT, ROPE, LATK = 512, 64, 576
SCALE2 = (128 + 64) ** -0.5 * 1.4426950408889634
FLOOR = -0.5e30
DEAD = -1e30
D = 7168
HALF = 896
KC = 256
GROUP = 512


def iota(shape, dim):
    return lax.broadcasted_iota(jnp.int32, shape, dim)


def dot(a, b):
    return jnp.dot(a, b, preferred_element_type=F32)


def kernel(
    slen,
    hid,
    newl,
    gain,
    gids,
    gwts,
    q_in,
    k_in,
    suf_in,
    vup_in,
    wo_in,
    wg_in,
    wu_in,
    wd_in,
    out_ref,
    q_own,
    q_all,
    place,
    qt,
    kt_own,
    kt_all,
    k_own,
    k_row,
    suf,
    nl,
    acc,
    mx,
    sm,
    vup,
    wo,
    wg,
    wu,
    wd,
    ctx,
    hv,
    hv_tx,
    hv_tw,
    st_own,
    st_tw,
    z_tx,
    z_rx,
    st_z,
    a_buf,
    a_rx,
    a_sum,
    a_in,
    ag,
    m_buf,
    m_rx,
    m_sum,
    m_in,
    ld,
    kss,
    krs,
    qss,
    qrs,
    qcs,
    qcr,
    near,
    far,
    tws,
    twr,
    tss,
    tsr,
    zss,
    zrs,
    zts,
    ztr,
    acs,
    acr,
    ars_s,
    ars_r,
    ags_s,
    ags_r,
    agc_s,
    agc_r,
    mcs,
    mcr,
    mrs_s,
    mrs_r,
):
    e = lax.axis_index("expert")
    r = lax.axis_index("resp")
    c = lax.rem(r, 2)
    z = r // 2
    right, left = lax.rem(e + 1, 4), lax.rem(e + 3, 4)
    twin = {"resp": z * 2 + 1 - c}

    def remote(src, dst, ssem, rsem, dev):
        return pltpu.make_async_remote_copy(
            src_ref=src, dst_ref=dst, send_sem=ssem, recv_sem=rsem, device_id=dev, device_id_type=MESH
        )

    def same_core(de, dz):
        return {"expert": lax.rem(e + de, 4), "resp": lax.rem(z + dz, 4) * 2 + c}

    loads = [
        pltpu.make_async_copy(q_in, q_own, ld.at[0]),
        pltpu.make_async_copy(k_in, kt_own, ld.at[1]),
        pltpu.make_async_copy(suf_in, suf, ld.at[2]),
        pltpu.make_async_copy(vup_in, vup, ld.at[3]),
        pltpu.make_async_copy(wo_in, wo, ld.at[4]),
        pltpu.make_async_copy(wg_in, wg, ld.at[5]),
        pltpu.make_async_copy(wu_in, wu, ld.at[6]),
        pltpu.make_async_copy(wd_in, wd, ld.at[7]),
    ]
    for x in loads[:3]:
        x.start()

    neighbours = [same_core(1, 0), same_core(3, 0), same_core(0, 1), same_core(0, 3), twin]
    bar = pltpu.get_barrier_semaphore()
    for x in neighbours:
        pl.semaphore_signal(bar, inc=1, device_id=x, device_id_type=MESH)
    loads[0].wait()
    q_all[r] = q_own[...].T
    pl.semaphore_wait(bar, 5)

    def k_send(src, j, d):
        dev = {"expert": right if d == 0 else left}
        return remote(src, kt_all.at[2 * j + d], kss.at[2 * j + d], krs.at[2 * j + d], dev)

    def own_chunk(j, d):
        return k_in.at[:, pl.ds(KC * (j if d == 0 else 3 - j), KC)]

    def k_forward(j, d):
        dev = {"expert": right if d == 0 else left}
        if j == 0:
            return [k_send(kt_all.at[d], 4, d)]
        sems = (10 + d, 12 + d)
        return [
            remote(
                kt_all.at[2 + d, :, pl.ds(128 * i, 128)],
                kt_all.at[10 + d, :, pl.ds(128 * i, 128)],
                kss.at[sems[i]],
                krs.at[sems[i]],
                dev,
            )
            for i in range(2)
        ]

    k_own_sends = [k_send(own_chunk(j, d), j, d) for j in range(4) for d in range(2)]

    def q_block(dz):
        return q_all.at[lax.rem(z + dz, 4) * 2 + c]

    half_rows = (pl.ds(0, LATK // 2), pl.ds(LATK // 2, LATK // 2))

    def q_send(i):
        if i < 2:
            part = q_block(0)
        else:
            part = q_block(3 if i == 2 else 1).at[half_rows[i - 2]]
        return remote(part, part, qss.at[i], qrs.at[i], same_core(0, 1 if i % 2 == 0 else 3))

    def q_come(i):
        if i < 2:
            part = q_block(3 if i == 0 else 1)
        else:
            part = q_block(2).at[half_rows[i - 2]]
        return remote(part, part, qss.at[i], qrs.at[i], same_core(0, 1 if i % 2 == 0 else 3))

    def q_cross(i):
        if i < 3:
            part = q_block((0, 3, 1)[i])
        else:
            part = q_block(2).at[half_rows[i - 3]]
        return remote(part, part, qcs.at[i], qcr.at[i], twin)

    def q_cross_come(i):
        if i < 3:
            part = q_all.at[lax.rem(z + (0, 3, 1)[i], 4) * 2 + 1 - c]
        else:
            part = q_all.at[lax.rem(z + 2, 4) * 2 + 1 - c].at[half_rows[i - 3]]
        return remote(part, part, qcs.at[i], qcr.at[i], twin)

    for x in k_own_sends[:2]:
        x.start()
    q_send(0).start()
    q_send(1).start()
    q_cross(0).start()
    for x in k_own_sends[2:]:
        x.start()
    for x in neighbours:
        pl.semaphore_signal(near, inc=1, device_id=x, device_id_type=MESH)

    mx[...] = jnp.full_like(mx, FLOOR)
    sm[...] = jnp.zeros_like(sm)
    acc[...] = jnp.zeros_like(acc)
    nl[...] = jnp.zeros_like(nl)
    nl[0:8, :] = newl[...]

    loads[1].wait()
    k_own[...] = kt_own[...].T

    def soft(s, g, vt):
        old = mx[g]
        new = jnp.maximum(old, jnp.max(s, axis=0, keepdims=True))
        mx[g] = new
        p = jnp.exp2((s - new) * SCALE2)
        shrink = jnp.exp2((old - new) * SCALE2)
        sm[g] = sm[g] * shrink + jnp.sum(p, axis=0, keepdims=True)
        acc[g] = acc[g] * shrink + dot(vt, p.astype(BF))

    row, col = iota((GROUP, GROUP), 0), iota((GROUP, GROUP), 1)
    want = ((col // 8) % 2) * 256 + (col % 8) * 32 + col // 16
    place[...] = jnp.where(row == want, 1.0, 0.0).astype(BF)

    def make_qt(g):
        block = jnp.concatenate([q_all[2 * g], q_all[2 * g + 1]], axis=1)
        qt[g] = dot(block, place[...]).astype(BF)

    def own_keys(g):
        s0 = dot(k_own[0:GROUP, :], qt[g])
        s1 = dot(k_own[GROUP : 2 * GROUP, :], qt[g])
        soft(s0, g, kt_own[0:LAT, 0:GROUP])
        soft(s1, g, kt_own[0:LAT, GROUP : 2 * GROUP])

    q_cross_come(0).wait_recv()
    make_qt(z)
    loads[2].wait()
    for x in loads[3:]:
        x.start()
    tok = iota((1, GROUP), 1) % 16
    mine = (tok // 8) == c
    for b in range(2):
        s = dot(suf[b].T, qt[z])
        live = (iota((GROUP, GROUP), 0) < slen[b]) & mine & ((tok % 8) // 4 == b)
        soft(jnp.where(live, s, DEAD), z, suf[b, 0:LAT, :])
    s = dot(nl[...], qt[z])
    key = iota((128, GROUP), 0)
    live = (key < 8) & mine & ((tok % 8) // 4 == key // 4) & (key % 4 <= tok % 4)
    soft(jnp.where(live, s, DEAD), z, nl[:, :LAT].T)
    own_keys(z)

    for i in range(2):
        q_come(i).wait_recv()
        q_cross(i + 1).start()
        q_send(i + 2).start()
    for i in range(2):
        g = lax.rem(z + (3, 1)[i], 4)
        q_cross_come(i + 1).wait_recv()
        make_qt(g)
        own_keys(g)
    for i in range(2):
        q_come(i + 2).wait_recv()
        q_cross(i + 3).start()
    for j in range(2):
        for d in range(2):
            k_send(kt_all.at[2 * j + d], j, d).wait_recv()
            for x in k_forward(j, d):
                x.start()
    for i in range(2):
        q_cross_come(i + 3).wait_recv()
    make_qt(lax.rem(z + 2, 4))
    own_keys(lax.rem(z + 2, 4))
    pl.semaphore_wait(near, 5)
    for x in (same_core(2, 0), same_core(0, 2)):
        pl.semaphore_signal(far, inc=1, device_id=x, device_id_type=MESH)

    def arrive(j):
        for d in range(2):
            k_send(kt_all.at[2 * j + d], j, d).wait_recv()

    def keys_of(pieces):
        at = 0
        for slot, first, width in pieces:
            k_row[at : at + width] = kt_all[slot, :, first : first + width].T
            at += width
        return jnp.concatenate([kt_all[slot, 0:LAT, first : first + width] for slot, first, width in pieces], axis=1)

    def groups(count, vt):
        s = dot(k_row[0:count], qt[0])
        for g in range(4):
            nxt = dot(k_row[0:count], qt[g + 1]) if g < 3 else None
            soft(s, g, vt)
            s = nxt

    def pair(j):
        vt = keys_of([(2 * j, 0, KC), (2 * j + 1, 0, KC)])
        groups(GROUP, vt)

    def pair_last(j, carry):
        arrive(j)
        pair(j)
        return carry

    pair(0)
    pair(1)
    lax.fori_loop(2, 5, pair_last, 0)
    for d in range(2):
        k_forward(1, d)[0].wait_recv()
    groups(KC, keys_of([(10, 0, 128), (11, 0, 128)]))
    pl.semaphore_wait(far, 2)
    loads[3].wait()
    for d in range(2):
        k_forward(1, d)[1].wait_recv()
    vt = keys_of([(10, 128, 128), (11, 128, 128)])

    def lanes_of(ref, q):
        return jnp.concatenate([ref[g, :, 128 * q : 128 * q + 128] for g in range(4)], axis=1)

    def last_scores(q):
        return dot(k_row[0:KC], lanes_of(qt, q))

    def finish(q, s):
        old = lanes_of(mx, q)
        new = jnp.maximum(old, jnp.max(s, axis=0, keepdims=True))
        p = jnp.exp2((s - new) * SCALE2)
        shrink = jnp.exp2((old - new) * SCALE2)
        total = lanes_of(sm, q) * shrink + jnp.sum(p, axis=0, keepdims=True)
        part = (lanes_of(acc, q) * shrink + dot(vt, p.astype(BF))) * (1.0 / total)
        st_own[q, 0:1, :] = new
        st_own[q, 1:2, :] = total
        ctx[q] = part.astype(BF).T.reshape(4, 8, 16, LAT)
        for h in range(8):
            hv[8 * q + h] = dot(ctx[q, :, h].reshape(64, LAT), vup[8 * q + h]).reshape(4, 16, 128)
        for g in range(4):
            block = hv[8 * q : 8 * q + 8, g].reshape(128, 128).T.astype(BF).reshape(4, 2, 16, 128)
            for cc in range(2):
                hv_tx[q, cc, :, :, 128 * g : 128 * g + 128] = block[:, cc]

    def twin_sends(q):
        return [
            remote(hv_tx.at[q, 1 - c], hv_tw.at[q], tws.at[q], twr.at[q], twin),
            remote(st_own.at[q], st_tw.at[q], tss.at[q], tsr.at[q], twin),
        ]

    def z_sends(q, dz):
        to = lax.rem(z + dz, 4)
        dev = same_core(0, dz)
        return [
            remote(z_tx.at[q, to], z_rx.at[q, dz], zss.at[q, dz], zrs.at[q, dz], dev),
            remote(st_z.at[q, 0], st_z.at[q, dz], zts.at[q, dz], ztr.at[q, dz], dev),
        ]

    def weight(st, top):
        return st[1:2, :] * jnp.exp2((st[0:1, :] - top) * SCALE2)

    def chip_sum(q):
        for x in twin_sends(q):
            x.wait_recv()
        top = jnp.maximum(st_own[q, 0:1, :], st_tw[q, 0:1, :])
        w1, w2 = weight(st_own[q], top), weight(st_tw[q], top)
        inv = 1.0 / (w1 + w2)
        mine = hv_tx[q, c].astype(F32) * (w1 * inv) + hv_tw[q].astype(F32) * (w2 * inv)
        z_tx[q] = mine.astype(BF)
        st_z[q, 0, 0:1, :] = top
        st_z[q, 0, 1:2, :] = w1 + w2
        for dz in (2, 1, 3):
            for x in z_sends(q, dz):
                x.start()

    def plane_sum(q):
        for dz in (2, 1, 3):
            for x in z_sends(q, dz):
                x.wait_recv()
        top = st_z[q, 0, 0:1, :]
        for dz in range(1, 4):
            top = jnp.maximum(top, st_z[q, dz, 0:1, :])
        w = [weight(st_z[q, dz], top) for dz in range(4)]
        y = z_tx[q, z].astype(F32) * w[0]
        for dz in range(1, 4):
            y = y + z_rx[q, dz].astype(F32) * w[dz]
        return (y * (1.0 / (w[0] + w[1] + w[2] + w[3]))).astype(BF)

    s = last_scores(0)
    for q in range(4):
        nxt = last_scores(q + 1) if q < 3 else None
        finish(q, s)
        for x in twin_sends(q):
            x.start()
        if q > 0:
            chip_sum(q - 1)
        s = nxt
    chip_sum(3)

    col, row = iota((GROUP, 64), 1), iota((GROUP, 64), 0)
    want = ((row % 16) // 8) * 32 + (row // 128) * 8 + row % 8
    gather = jnp.where(col == want, 1.0, 0.0).astype(BF)
    keep = (iota((128, GROUP), 0) // 16) == ((iota((128, GROUP), 1) % 128) // 16)
    lhs = []
    for hb in range(4):
        piece = plane_sum(hb)
        piece = jnp.concatenate([piece] * 8, axis=0)
        lhs.append(dot(jnp.where(keep, piece, jnp.zeros_like(piece)), gather))
    lhs = jnp.concatenate(lhs, axis=0).T.astype(BF)

    def core_send(buf, rx, ssem, rsem, x):
        return remote(buf.at[1 - c, x], rx.at[x], ssem.at[x], rsem.at[x], twin)

    def scatter_send(total_buf, landing, ssem, rsem, de, dz):
        src = total_buf.at[lax.rem(e + de, 4), lax.rem(z + dz, 4)]
        i = dz * 4 + de
        return remote(src, landing.at[i], ssem.at[i], rsem.at[i], same_core(de, dz))

    def shares(h, tile, buf, rx, cs, cr):
        for de in (2, 1, 3, 0):
            x = lax.rem(e + de, 4)
            terms = tile(x)
            for g in range(4):
                rows = terms[8 * g : 8 * g + 8, :]
                buf[h, x, g] = jnp.concatenate([rows[:, :HALF], rows[:, HALF:]], axis=0).astype(BF)

            @pl.when(c != h)
            def _():
                core_send(buf, rx, cs, cr, x).start()

    def pass_on(h, buf, rx, total_buf, landing, cs, cr, ss, sr):
        @pl.when(c == h)
        def _():
            for de in (2, 1, 3, 0):
                x = lax.rem(e + de, 4)
                core_send(buf, rx, cs, cr, x).wait_recv()
                total_buf[x] = (buf[h, x].astype(F32) + rx[x].astype(F32)).astype(BF)
                for dz in (2, 1, 3, 0):
                    if de or dz:
                        scatter_send(total_buf, landing, ss, sr, de, dz).start()

    def collect(total_buf, landing, ss, sr):
        out = total_buf[e, z].astype(F32)
        for de in (2, 1, 3, 0):
            for dz in (2, 1, 3, 0):
                if de or dz:
                    scatter_send(total_buf, landing, ss, sr, de, dz).wait_recv()
                    out = out + landing[dz * 4 + de].astype(F32)
        return out

    def columns(x):
        return pl.ds(pl.multiple_of(x * 1792, 128), 1792)

    loads[4].wait()
    for h in range(2):
        shares(h, lambda x: dot(lhs[32 * h : 32 * h + 32], wo[:, columns(x)]), a_buf, a_rx, acs, acr)
        pass_on(h, a_buf, a_rx, a_sum, a_in, acs, acr, ars_s, ars_r)

    def ag_send(de, dz):
        i = dz * 4 + de
        return remote(ag.at[c, e, z], ag.at[c, e, z], ags_s.at[i], ags_r.at[i], same_core(de, dz))

    def ag_cross(x):
        return remote(ag.at[c, x], ag.at[c, x], agc_s.at[x], agc_r.at[x], twin)

    def ag_cross_come(x):
        return remote(ag.at[1 - c, x], ag.at[1 - c, x], agc_s.at[x], agc_r.at[x], twin)

    def residual(h):
        @pl.when(c == h)
        def _():
            attended = collect(a_sum, a_in, ars_s, ars_r).astype(BF)
            hidden = jnp.concatenate([hid[:, :HALF], hid[:, HALF:]], axis=0)
            ag[h, e, z] = (hidden.astype(F32) + attended.astype(F32)).astype(BF)
            for de in (0, 1, 3, 2):
                for dz in range(4):
                    if de or dz:
                        ag_send(de, dz).start()
            out_ref[0] = jnp.concatenate([attended[0:8], attended[8:16]], axis=1)

    residual(0)
    residual(1)

    picked = jnp.where(gids[...] == e, gwts[...], 0.0)
    share = 2.5 * jnp.sum(picked, axis=0, keepdims=True) / jnp.sum(gwts[...], axis=0, keepdims=True)
    row, tok = iota((64, 64), 0), iota((64, 64), 1)
    here = tok == ((row // 8) % 4) * 16 + (row // 32) * 8 + row % 8
    share = jnp.sum(jnp.where(here, share, 0.0), axis=1, keepdims=True)
    loads[5].wait()
    loads[6].wait()
    loads[7].wait()

    def experts(h):
        squares = jnp.zeros((32, 1), F32)
        gate = jnp.zeros((32, 256), F32)
        up = jnp.zeros((32, 256), F32)
        for de in (0, 1, 3, 2):
            x = lax.rem(e + 4 - de, 4)

            @pl.when(c == h)
            def _():
                for dz in range(4):
                    if de or dz:
                        ag_send(de, dz).wait_recv()
                ag_cross(x).start()

            @pl.when(c != h)
            def _():
                ag_cross_come(x).wait_recv()

            wide = ag[h, x].astype(F32)
            for half in range(2):
                part = wide[:, 8 * half : 8 * half + 8, :].reshape(32, HALF)
                squares = squares + jnp.sum(part * part, axis=1, keepdims=True)
                scaled = (part * gain[2 * x + half]).astype(BF)
                rows = pl.ds(pl.multiple_of(x * 1792 + half * HALF, HALF), HALF)
                gate = gate + dot(scaled, wg[rows, :])
                up = up + dot(scaled, wu[rows, :])
        norm = lax.rsqrt(squares * (1.0 / D) + 1e-6)
        gate = gate * norm
        up = up * norm
        act = (gate / (1.0 + jnp.exp(-gate)) * up).astype(BF)
        part = share[32 * h : 32 * h + 32]
        shares(h, lambda x: dot(act, wd[:, columns(x)]) * part, m_buf, m_rx, mcs, mcr)
        pass_on(h, m_buf, m_rx, m_sum, m_in, mcs, mcr, mrs_s, mrs_r)

    experts(0)
    experts(1)
    moe = collect(m_sum, m_in, mrs_s, mrs_r)
    out = (ag[c, e, z].astype(F32) + moe).astype(BF)
    out_ref[1] = jnp.concatenate([out[0:8], out[8:16]], axis=1)

    for x in k_own_sends:
        x.wait_send()
    for j in range(2):
        for d in range(2):
            for x in k_forward(j, d):
                x.wait_send()
    for i in range(4):
        q_send(i).wait_send()
    for i in range(5):
        q_cross(i).wait_send()
    for q in range(4):
        for x in twin_sends(q):
            x.wait_send()
        for dz in range(1, 4):
            for x in z_sends(q, dz):
                x.wait_send()
    for x in range(4):
        core_send(a_buf, a_rx, acs, acr, x).wait_send()
        core_send(m_buf, m_rx, mcs, mcr, x).wait_send()
        ag_cross(x).wait_send()
    for i in range(1, 16):
        scatter_send(a_sum, a_in, ars_s, ars_r, i % 4, i // 4).wait_send()
        scatter_send(m_sum, m_in, mrs_s, mrs_r, i % 4, i // 4).wait_send()
        ag_send(i % 4, i // 4).wait_send()


def on_device(
    hidden,
    queries,
    new_latents,
    suffix_cache,
    suffix_lengths,
    prompt_latents,
    value_up,
    out_proj,
    rms_gain,
    gate_ids,
    gate_weights,
    w_gate,
    w_up,
    w_down,
):
    any_spec = pl.BlockSpec(memory_space=pl.ANY)
    vmem = pl.BlockSpec(memory_space=pltpu.VMEM)
    smem = pl.BlockSpec(memory_space=pltpu.SMEM)
    sem = pltpu.SemaphoreType.DMA
    out = jax.ShapeDtypeStruct((2, 8, 1792), BF)
    block = (16, HALF)
    scratch = [
        pltpu.VMEM((256, LATK), BF),
        pltpu.VMEM((8, LATK, 256), BF),
        pltpu.VMEM((GROUP, GROUP), BF),
        pltpu.VMEM((4, LATK, GROUP), BF),
        pltpu.VMEM((LATK, 1024), BF),
        pltpu.VMEM((12, LATK, KC), BF),
        pltpu.VMEM((1024, LATK), BF),
        pltpu.VMEM((GROUP, LATK), BF),
        pltpu.VMEM((2, LATK, GROUP), BF),
        pltpu.VMEM((128, LATK), BF),
        pltpu.VMEM((4, LAT, GROUP), F32),
        pltpu.VMEM((4, 1, GROUP), F32),
        pltpu.VMEM((4, 1, GROUP), F32),
        pltpu.VMEM((32, LAT, 128), BF),
        pltpu.VMEM((512, D), BF),
        pltpu.VMEM((D, 256), BF),
        pltpu.VMEM((D, 256), BF),
        pltpu.VMEM((256, D), BF),
        pltpu.VMEM((4, 4, 8, 16, LAT), BF),
        pltpu.VMEM((32, 4, 16, 128), F32),
        pltpu.VMEM((4, 2, 4, 16, GROUP), BF),
        pltpu.VMEM((4, 4, 16, GROUP), BF),
        pltpu.VMEM((4, 2, GROUP), F32),
        pltpu.VMEM((4, 2, GROUP), F32),
        pltpu.VMEM((4, 4, 16, GROUP), BF),
        pltpu.VMEM((4, 4, 16, GROUP), BF),
        pltpu.VMEM((4, 4, 2, GROUP), F32),
        pltpu.VMEM((2, 4, 4) + block, BF),
        pltpu.VMEM((4, 4) + block, BF),
        pltpu.VMEM((4, 4) + block, BF),
        pltpu.VMEM((16,) + block, BF),
        pltpu.VMEM((2, 4, 4) + block, BF),
        pltpu.VMEM((2, 4, 4) + block, BF),
        pltpu.VMEM((4, 4) + block, BF),
        pltpu.VMEM((4, 4) + block, BF),
        pltpu.VMEM((16,) + block, BF),
    ]
    scratch += [sem((n,)) for n in (8, 14, 14, 4, 4, 5, 5)]
    scratch += [pltpu.SemaphoreType.REGULAR, pltpu.SemaphoreType.REGULAR]
    scratch += [sem((4,))] * 4 + [sem((4, 4))] * 4
    scratch += [sem((n,)) for n in (4, 4, 16, 16, 16, 16, 4, 4, 4, 4, 16, 16)]
    both = pl.pallas_call(
        kernel,
        out_shape=out,
        in_specs=[smem] + [vmem] * 5 + [any_spec] * 8,
        out_specs=vmem,
        scratch_shapes=scratch,
        compiler_params=pltpu.CompilerParams(
            collective_id=0, has_side_effects=True, vmem_limit_bytes=62 * 2**20
        ),
    )(
        suffix_lengths,
        hidden,
        new_latents,
        rms_gain.reshape(8, 1, HALF),
        gate_ids.T,
        gate_weights.T,
        queries.reshape(256, LATK),
        prompt_latents.T,
        jnp.swapaxes(suffix_cache, 1, 2),
        value_up,
        out_proj.reshape(512, D),
        w_gate[0],
        w_up[0],
        w_down[0],
    )
    return both[0], both[1]


def solution(mesh):
    placed = (
        P(("prompt", "resp"), "expert"),
        P(("prompt", "resp"), "expert", None),
        P(("prompt", "resp"), None),
        P(("prompt", "resp"), None, None),
        P(("prompt", "resp")),
        P(("prompt", "resp", "expert"), None),
        P("expert", None, None),
        P("expert", "resp", None),
        P(),
        P("prompt", None),
        P("prompt", None),
        P("expert", None, "resp"),
        P("expert", None, "resp"),
        P("expert", "resp", None),
    )
    return jax.shard_map(
        on_device,
        mesh=mesh,
        in_specs=placed,
        out_specs=(P(("prompt", "resp"), "expert"), P(("prompt", "resp"), "expert")),
        check_vma=False,
    )
```

```python
import jax
import jax.numpy as jnp
from jax import lax
from jax.experimental import pallas as pl
from jax.experimental.pallas import tpu as pltpu
from jax.sharding import PartitionSpec as P

MESH = pl.DeviceIdType.MESH
BF = jnp.bfloat16
F32 = jnp.float32
LAT, ROPE, LATK = 512, 64, 576
SCALE2 = (128 + 64) ** -0.5 * 1.4426950408889634
FLOOR = -0.5e30
DEAD = -1e30
D = 7168
HALF = 896
KC = 256
GROUP = 512


def iota(shape, dim):
    return lax.broadcasted_iota(jnp.int32, shape, dim)


def dot(a, b):
    return jnp.dot(a, b, preferred_element_type=F32)


def kernel(
    slen,
    hid,
    newl,
    gain,
    gids,
    gwts,
    q_in,
    k_in,
    suf_in,
    vup_in,
    wo_in,
    wg_in,
    wu_in,
    wd_in,
    out_ref,
    q_own,
    q_all,
    place,
    qt,
    kt_own,
    kt_all,
    k_own,
    k_row,
    suf,
    nl,
    acc,
    mx,
    sm,
    vup,
    wo,
    wg,
    wu,
    wd,
    ctx,
    hv,
    hv_tx,
    hv_tw,
    st_own,
    st_tw,
    z_tx,
    z_rx,
    st_z,
    d_rx,
    d_st,
    a_old,
    a_buf,
    a_rx,
    a_sum,
    a_in,
    ag,
    m_buf,
    m_rx,
    m_sum,
    m_in,
    ld,
    kss,
    krs,
    qss,
    qrs,
    qcs,
    qcr,
    near,
    far,
    tws,
    twr,
    tss,
    tsr,
    zss,
    zrs,
    zts,
    ztr,
    dss,
    dsr,
    dts,
    dtr,
    acs,
    acr,
    ars_s,
    ars_r,
    ags_s,
    ags_r,
    agc_s,
    agc_r,
    mcs,
    mcr,
    mrs_s,
    mrs_r,
):
    e = lax.axis_index("expert")
    r = lax.axis_index("resp")
    c = lax.rem(r, 2)
    z = r // 2
    right, left = lax.rem(e + 1, 4), lax.rem(e + 3, 4)
    twin = {"resp": z * 2 + 1 - c}

    def remote(src, dst, ssem, rsem, dev):
        return pltpu.make_async_remote_copy(
            src_ref=src, dst_ref=dst, send_sem=ssem, recv_sem=rsem, device_id=dev, device_id_type=MESH
        )

    def same_core(de, dz):
        return {"expert": lax.rem(e + de, 4), "resp": lax.rem(z + dz, 4) * 2 + c}

    loads = [
        pltpu.make_async_copy(q_in, q_own, ld.at[0]),
        pltpu.make_async_copy(k_in, kt_own, ld.at[1]),
        pltpu.make_async_copy(suf_in, suf, ld.at[2]),
        pltpu.make_async_copy(vup_in, vup, ld.at[3]),
        pltpu.make_async_copy(wo_in, wo, ld.at[4]),
        pltpu.make_async_copy(wg_in, wg, ld.at[5]),
        pltpu.make_async_copy(wu_in, wu, ld.at[6]),
        pltpu.make_async_copy(wd_in, wd, ld.at[7]),
    ]
    for i in (1, 0, 2):
        loads[i].start()

    neighbours = [same_core(1, 0), same_core(3, 0), same_core(0, 1), same_core(0, 3), twin]
    bar = pltpu.get_barrier_semaphore()
    for x in neighbours:
        pl.semaphore_signal(bar, inc=1, device_id=x, device_id_type=MESH)
    loads[0].wait()
    q_all[r] = q_own[...].T
    loads[1].wait()
    pl.semaphore_wait(bar, 5)

    def k_send(src, j, d):
        dev = {"expert": right if d == 0 else left}
        return remote(src, kt_all.at[2 * j + d], kss.at[2 * j + d], krs.at[2 * j + d], dev)

    def own_chunk(j, d):
        return kt_own.at[:, pl.ds(KC * (j if d == 0 else 3 - j), KC)]

    def k_forward(j, d):
        dev = {"expert": right if d == 0 else left}
        if j == 0:
            return [k_send(kt_all.at[d], 4, d)]
        sems = (10 + d, 12 + d)
        return [
            remote(
                kt_all.at[2 + d, :, pl.ds(128 * i, 128)],
                kt_all.at[10 + d, :, pl.ds(128 * i, 128)],
                kss.at[sems[i]],
                krs.at[sems[i]],
                dev,
            )
            for i in range(2)
        ]

    k_own_sends = [k_send(own_chunk(j, d), j, d) for j in range(4) for d in range(2)]

    def q_block(dz):
        return q_all.at[lax.rem(z + dz, 4) * 2 + c]

    half_rows = (pl.ds(0, LATK // 2), pl.ds(LATK // 2, LATK // 2))

    def q_send(i):
        if i < 2:
            part = q_block(0)
        else:
            part = q_block(3 if i == 2 else 1).at[half_rows[i - 2]]
        return remote(part, part, qss.at[i], qrs.at[i], same_core(0, 1 if i % 2 == 0 else 3))

    def q_come(i):
        if i < 2:
            part = q_block(3 if i == 0 else 1)
        else:
            part = q_block(2).at[half_rows[i - 2]]
        return remote(part, part, qss.at[i], qrs.at[i], same_core(0, 1 if i % 2 == 0 else 3))

    def q_cross(i):
        if i < 3:
            part = q_block((0, 3, 1)[i])
        else:
            part = q_block(2).at[half_rows[i - 3]]
        return remote(part, part, qcs.at[i], qcr.at[i], twin)

    def q_cross_come(i):
        if i < 3:
            part = q_all.at[lax.rem(z + (0, 3, 1)[i], 4) * 2 + 1 - c]
        else:
            part = q_all.at[lax.rem(z + 2, 4) * 2 + 1 - c].at[half_rows[i - 3]]
        return remote(part, part, qcs.at[i], qcr.at[i], twin)

    for x in k_own_sends[:2]:
        x.start()
    q_send(0).start()
    q_send(1).start()
    q_cross(0).start()
    for x in k_own_sends[2:]:
        x.start()
    for x in neighbours:
        pl.semaphore_signal(near, inc=1, device_id=x, device_id_type=MESH)

    mx[...] = jnp.full_like(mx, FLOOR)
    sm[...] = jnp.zeros_like(sm)
    acc[...] = jnp.zeros_like(acc)
    nl[...] = jnp.zeros_like(nl)
    nl[0:8, :] = newl[...]

    k_own[...] = kt_own[...].T

    def soft(s, g, vt):
        old = mx[g]
        new = jnp.maximum(old, jnp.max(s, axis=0, keepdims=True))
        mx[g] = new
        p = jnp.exp2((s - new) * SCALE2)
        shrink = jnp.exp2((old - new) * SCALE2)
        sm[g] = sm[g] * shrink + jnp.sum(p, axis=0, keepdims=True)
        acc[g] = acc[g] * shrink + dot(vt, p.astype(BF))

    row, col = iota((GROUP, GROUP), 0), iota((GROUP, GROUP), 1)
    want = ((col // 8) % 2) * 256 + (col % 8) * 32 + col // 16
    place[...] = jnp.where(row == want, 1.0, 0.0).astype(BF)

    def make_qt(g):
        block = jnp.concatenate([q_all[2 * g], q_all[2 * g + 1]], axis=1)
        qt[g] = dot(block, place[...]).astype(BF)

    def own_keys(g):
        s0 = dot(k_own[0:GROUP, :], qt[g])
        s1 = dot(k_own[GROUP : 2 * GROUP, :], qt[g])
        soft(s0, g, kt_own[0:LAT, 0:GROUP])
        soft(s1, g, kt_own[0:LAT, GROUP : 2 * GROUP])

    q_cross_come(0).wait_recv()
    make_qt(z)
    loads[2].wait()
    for x in loads[3:]:
        x.start()
    tok = iota((1, GROUP), 1) % 16
    mine = (tok // 8) == c
    for b in range(2):
        s = dot(suf[b].T, qt[z])
        live = (iota((GROUP, GROUP), 0) < slen[b]) & mine & ((tok % 8) // 4 == b)
        soft(jnp.where(live, s, DEAD), z, suf[b, 0:LAT, :])
    s = dot(nl[...], qt[z])
    key = iota((128, GROUP), 0)
    live = (key < 8) & mine & ((tok % 8) // 4 == key // 4) & (key % 4 <= tok % 4)
    soft(jnp.where(live, s, DEAD), z, nl[:, :LAT].T)
    own_keys(z)

    for i in range(2):
        q_come(i).wait_recv()
        q_cross(i + 1).start()
        q_send(i + 2).start()
    for i in range(2):
        g = lax.rem(z + (3, 1)[i], 4)
        q_cross_come(i + 1).wait_recv()
        make_qt(g)
        own_keys(g)
    for i in range(2):
        q_come(i + 2).wait_recv()
        q_cross(i + 3).start()
    for j in range(2):
        for d in range(2):
            k_send(kt_all.at[2 * j + d], j, d).wait_recv()
            for x in k_forward(j, d):
                x.start()
    for i in range(2):
        q_cross_come(i + 3).wait_recv()
    make_qt(lax.rem(z + 2, 4))
    own_keys(lax.rem(z + 2, 4))
    pl.semaphore_wait(near, 5)
    for x in (same_core(2, 0), same_core(0, 2)):
        pl.semaphore_signal(far, inc=1, device_id=x, device_id_type=MESH)

    def arrive(j):
        for d in range(2):
            k_send(kt_all.at[2 * j + d], j, d).wait_recv()

    def keys_of(pieces):
        at = 0
        for slot, first, width in pieces:
            k_row[at : at + width] = kt_all[slot, :, first : first + width].T
            at += width
        return jnp.concatenate([kt_all[slot, 0:LAT, first : first + width] for slot, first, width in pieces], axis=1)

    def groups(count, vt):
        s = dot(k_row[0:count], qt[0])
        for g in range(4):
            nxt = dot(k_row[0:count], qt[g + 1]) if g < 3 else None
            soft(s, g, vt)
            s = nxt

    def pair(j):
        vt = keys_of([(2 * j, 0, KC), (2 * j + 1, 0, KC)])
        groups(GROUP, vt)

    def pair_last(j, carry):
        arrive(j)
        pair(j)
        return carry

    pair(0)
    pair(1)
    lax.fori_loop(2, 5, pair_last, 0)
    for d in range(2):
        k_forward(1, d)[0].wait_recv()
    groups(KC, keys_of([(10, 0, 128), (11, 0, 128)]))
    pl.semaphore_wait(far, 2)
    loads[3].wait()
    for d in range(2):
        k_forward(1, d)[1].wait_recv()
    vt = keys_of([(10, 128, 128), (11, 128, 128)])

    def lanes_of(ref, q):
        return jnp.concatenate([ref[g, :, 128 * q : 128 * q + 128] for g in range(4)], axis=1)

    def last_scores(q):
        return dot(k_row[0:KC], lanes_of(qt, q))

    def finish(q, s):
        old = lanes_of(mx, q)
        new = jnp.maximum(old, jnp.max(s, axis=0, keepdims=True))
        p = jnp.exp2((s - new) * SCALE2)
        shrink = jnp.exp2((old - new) * SCALE2)
        total = lanes_of(sm, q) * shrink + jnp.sum(p, axis=0, keepdims=True)
        part = (lanes_of(acc, q) * shrink + dot(vt, p.astype(BF))) * (1.0 / total)
        st_own[q, 0:1, :] = new
        st_own[q, 1:2, :] = total
        ctx[q] = part.astype(BF).T.reshape(4, 8, 16, LAT)
        for h in range(8):
            hv[8 * q + h] = dot(ctx[q, :, h].reshape(64, LAT), vup[8 * q + h]).reshape(4, 16, 128)
        for g in range(4):
            block = hv[8 * q : 8 * q + 8, g].reshape(128, 128).T.astype(BF).reshape(4, 2, 16, 128)
            for cc in range(2):
                hv_tx[q, cc, :, :, 128 * g : 128 * g + 128] = block[:, cc]

    def twin_sends(q):
        return [
            remote(hv_tx.at[q, 1 - c], hv_tw.at[q], tws.at[q], twr.at[q], twin),
            remote(st_own.at[q], st_tw.at[q], tss.at[q], tsr.at[q], twin),
        ]

    def z_sends(q, dz):
        to = lax.rem(z + dz, 4)
        dev = same_core(0, dz)
        return [
            remote(z_tx.at[q, to], z_rx.at[q, dz], zss.at[q, dz], zrs.at[q, dz], dev),
            remote(st_z.at[q, 0], st_z.at[q, dz], zts.at[q, dz], ztr.at[q, dz], dev),
        ]

    def direct_sends(i):
        to = lax.rem(r + i, 8)
        dev = {"resp": to}
        return [
            remote(hv_tx.at[3, lax.rem(to, 2), to // 2], d_rx.at[i], dss.at[i], dsr.at[i], dev),
            remote(st_own.at[3], d_st.at[i], dts.at[i], dtr.at[i], dev),
        ]

    def weight(st, top):
        return st[1:2, :] * jnp.exp2((st[0:1, :] - top) * SCALE2)

    def chip_sum(q):
        for x in twin_sends(q):
            x.wait_recv()
        top = jnp.maximum(st_own[q, 0:1, :], st_tw[q, 0:1, :])
        w1, w2 = weight(st_own[q], top), weight(st_tw[q], top)
        inv = 1.0 / (w1 + w2)
        mine = hv_tx[q, c].astype(F32) * (w1 * inv) + hv_tw[q].astype(F32) * (w2 * inv)
        z_tx[q] = mine.astype(BF)
        st_z[q, 0, 0:1, :] = top
        st_z[q, 0, 1:2, :] = w1 + w2
        for dz in (2, 1, 3):
            for x in z_sends(q, dz):
                x.start()

    def plane_sum(q):
        for dz in (2, 1, 3):
            for x in z_sends(q, dz):
                x.wait_recv()
        top = st_z[q, 0, 0:1, :]
        for dz in range(1, 4):
            top = jnp.maximum(top, st_z[q, dz, 0:1, :])
        w = [weight(st_z[q, dz], top) for dz in range(4)]
        y = z_tx[q, z].astype(F32) * w[0]
        for dz in range(1, 4):
            y = y + z_rx[q, dz].astype(F32) * w[dz]
        return (y * (1.0 / (w[0] + w[1] + w[2] + w[3]))).astype(BF)

    def plane_sum_direct():
        for i in (1, 7, 2, 6, 3, 5, 4):
            for x in direct_sends(i):
                x.wait_recv()
        top = st_own[3, 0:1, :]
        for i in range(1, 8):
            top = jnp.maximum(top, d_st[i, 0:1, :])
        total = weight(st_own[3], top)
        y = hv_tx[3, c, z].astype(F32) * total
        for i in range(1, 8):
            w = weight(d_st[i], top)
            total = total + w
            y = y + d_rx[i].astype(F32) * w
        return (y * (1.0 / total)).astype(BF)

    s = last_scores(0)
    for q in range(4):
        nxt = last_scores(q + 1) if q < 3 else None
        finish(q, s)
        if q < 3:
            for x in twin_sends(q):
                x.start()
        else:
            for i in (4, 3, 5, 2, 6, 1, 7):
                for x in direct_sends(i):
                    x.start()
        if q > 0:
            chip_sum(q - 1)
        s = nxt

    col, row = iota((GROUP, 64), 1), iota((GROUP, 64), 0)
    want = ((row % 16) // 8) * 32 + (row // 128) * 8 + row % 8
    gather = jnp.where(col == want, 1.0, 0.0).astype(BF)
    keep = (iota((128, GROUP), 0) // 16) == ((iota((128, GROUP), 1) % 128) // 16)

    def spread(y):
        y = jnp.concatenate([y] * 8, axis=0)
        return dot(jnp.where(keep, y, jnp.zeros_like(y)), gather).T.astype(BF)

    def columns(x):
        return pl.ds(pl.multiple_of(x * 1792, 128), 1792)

    loads[4].wait()
    early = jnp.concatenate([spread(plane_sum(q)) for q in range(3)], axis=1)
    for x in range(4):
        a_old[x] = dot(early, wo[0:384, 1792 * x : 1792 * (x + 1)])
    late = spread(plane_sum_direct())

    def core_send(buf, rx, ssem, rsem, x):
        return remote(buf.at[1 - c, x], rx.at[x], ssem.at[x], rsem.at[x], twin)

    def scatter_send(total_buf, landing, ssem, rsem, de, dz):
        src = total_buf.at[lax.rem(e + de, 4), lax.rem(z + dz, 4)]
        i = dz * 4 + de
        return remote(src, landing.at[i], ssem.at[i], rsem.at[i], same_core(de, dz))

    def fill(buf, x, tile):
        for cc in range(2):
            for g in range(4):
                rows = tile[32 * cc + 8 * g : 32 * cc + 8 * g + 8, :]
                buf[cc, x, g] = jnp.concatenate([rows[:, :HALF], rows[:, HALF:]], axis=0).astype(BF)

    def reduce_scatter(tile, buf, rx, total_buf, landing, cs, cr, ss, sr):
        def pass_on(de):
            x = lax.rem(e + de, 4)
            core_send(buf, rx, cs, cr, x).wait_recv()
            total_buf[x] = (buf[c, x].astype(F32) + rx[x].astype(F32)).astype(BF)
            for dz in (2, 1, 3, 0):
                if de or dz:
                    scatter_send(total_buf, landing, ss, sr, de, dz).start()

        last = None
        for de in (2, 1, 3, 0):
            x = lax.rem(e + de, 4)
            fill(buf, x, tile(x))
            core_send(buf, rx, cs, cr, x).start()
            if last is not None:
                pass_on(last)
            last = de
        pass_on(last)
        out = total_buf[e, z].astype(F32)
        for de in (0, 1, 3, 2):
            for dz in (0, 1, 3, 2):
                if de or dz:
                    scatter_send(total_buf, landing, ss, sr, de, dz).wait_recv()
                    out = out + landing[dz * 4 + de].astype(F32)
        return out

    attended = reduce_scatter(
        lambda x: a_old[x] + dot(late, wo[384:512, columns(x)]), a_buf, a_rx, a_sum, a_in, acs, acr, ars_s, ars_r
    ).astype(BF)
    hidden = jnp.concatenate([hid[:, :HALF], hid[:, HALF:]], axis=0)
    resid = (hidden.astype(F32) + attended.astype(F32)).astype(BF)
    ag[c, e, z] = resid
    out_ref[0] = jnp.concatenate([attended[0:8], attended[8:16]], axis=1)

    def ag_send(de, dz):
        i = dz * 4 + de
        return remote(ag.at[c, e, z], ag.at[c, e, z], ags_s.at[i], ags_r.at[i], same_core(de, dz))

    def ag_cross(x):
        return remote(ag.at[c, x], ag.at[c, x], agc_s.at[x], agc_r.at[x], twin)

    for de in (2, 1, 3, 0):
        for dz in (2, 1, 3, 0):
            if de or dz:
                ag_send(de, dz).start()

    loads[5].wait()
    loads[6].wait()
    squares = jnp.zeros((64, 1), F32)
    gate = jnp.zeros((64, 256), F32)
    up = jnp.zeros((64, 256), F32)
    def features(de, squares, gate, up):
        x = lax.rem(e + 4 - de, 4)
        ag_cross(x).wait_recv()
        wide = ag[:, x].astype(F32)
        for half in range(2):
            part = wide[:, :, 8 * half : 8 * half + 8, :].reshape(64, HALF)
            squares = squares + jnp.sum(part * part, axis=1, keepdims=True)
            scaled = (part * gain[2 * x + half]).astype(BF)
            rows = pl.ds(pl.multiple_of(x * 1792 + half * HALF, HALF), HALF)
            gate = gate + dot(scaled, wg[rows, :])
            up = up + dot(scaled, wu[rows, :])
        return squares, gate, up

    last = None
    for de in (2, 1, 3, 0):
        for dz in range(4):
            if de or dz:
                ag_send(de, dz).wait_recv()
        ag_cross(lax.rem(e + 4 - de, 4)).start()
        if last is not None:
            squares, gate, up = features(last, squares, gate, up)
        last = de
    squares, gate, up = features(last, squares, gate, up)
    norm = lax.rsqrt(squares * (1.0 / D) + 1e-6)
    gate = gate * norm
    up = up * norm
    act = (gate / (1.0 + jnp.exp(-gate)) * up).astype(BF)

    picked = jnp.where(gids[...] == e, gwts[...], 0.0)
    share = 2.5 * jnp.sum(picked, axis=0, keepdims=True) / jnp.sum(gwts[...], axis=0, keepdims=True)
    row, tok = iota((64, 64), 0), iota((64, 64), 1)
    here = tok == ((row // 8) % 4) * 16 + (row // 32) * 8 + row % 8
    share = jnp.sum(jnp.where(here, share, 0.0), axis=1, keepdims=True)
    loads[7].wait()
    moe = reduce_scatter(
        lambda x: dot(act, wd[:, columns(x)]) * share, m_buf, m_rx, m_sum, m_in, mcs, mcr, mrs_s, mrs_r
    )
    out = (resid.astype(F32) + moe).astype(BF)
    out_ref[1] = jnp.concatenate([out[0:8], out[8:16]], axis=1)

    for x in k_own_sends:
        x.wait_send()
    for j in range(2):
        for d in range(2):
            for x in k_forward(j, d):
                x.wait_send()
    for i in range(4):
        q_send(i).wait_send()
    for i in range(5):
        q_cross(i).wait_send()
    for i in range(1, 8):
        for x in direct_sends(i):
            x.wait_send()
    for q in range(3):
        for x in twin_sends(q):
            x.wait_send()
        for dz in range(1, 4):
            for x in z_sends(q, dz):
                x.wait_send()
    for x in range(4):
        core_send(a_buf, a_rx, acs, acr, x).wait_send()
        core_send(m_buf, m_rx, mcs, mcr, x).wait_send()
        ag_cross(x).wait_send()
    for i in range(1, 16):
        scatter_send(a_sum, a_in, ars_s, ars_r, i % 4, i // 4).wait_send()
        scatter_send(m_sum, m_in, mrs_s, mrs_r, i % 4, i // 4).wait_send()
        ag_send(i % 4, i // 4).wait_send()


def on_device(
    hidden,
    queries,
    new_latents,
    suffix_cache,
    suffix_lengths,
    prompt_latents,
    value_up,
    out_proj,
    rms_gain,
    gate_ids,
    gate_weights,
    w_gate,
    w_up,
    w_down,
):
    any_spec = pl.BlockSpec(memory_space=pl.ANY)
    vmem = pl.BlockSpec(memory_space=pltpu.VMEM)
    smem = pl.BlockSpec(memory_space=pltpu.SMEM)
    sem = pltpu.SemaphoreType.DMA
    out = jax.ShapeDtypeStruct((2, 8, 1792), BF)
    block = (16, HALF)
    scratch = [
        pltpu.VMEM((256, LATK), BF),
        pltpu.VMEM((8, LATK, 256), BF),
        pltpu.VMEM((GROUP, GROUP), BF),
        pltpu.VMEM((4, LATK, GROUP), BF),
        pltpu.VMEM((LATK, 1024), BF),
        pltpu.VMEM((12, LATK, KC), BF),
        pltpu.VMEM((1024, LATK), BF),
        pltpu.VMEM((GROUP, LATK), BF),
        pltpu.VMEM((2, LATK, GROUP), BF),
        pltpu.VMEM((128, LATK), BF),
        pltpu.VMEM((4, LAT, GROUP), F32),
        pltpu.VMEM((4, 1, GROUP), F32),
        pltpu.VMEM((4, 1, GROUP), F32),
        pltpu.VMEM((32, LAT, 128), BF),
        pltpu.VMEM((512, D), BF),
        pltpu.VMEM((D, 256), BF),
        pltpu.VMEM((D, 256), BF),
        pltpu.VMEM((256, D), BF),
        pltpu.VMEM((4, 4, 8, 16, LAT), BF),
        pltpu.VMEM((32, 4, 16, 128), F32),
        pltpu.VMEM((4, 2, 4, 16, GROUP), BF),
        pltpu.VMEM((4, 4, 16, GROUP), BF),
        pltpu.VMEM((4, 2, GROUP), F32),
        pltpu.VMEM((4, 2, GROUP), F32),
        pltpu.VMEM((4, 4, 16, GROUP), BF),
        pltpu.VMEM((4, 4, 16, GROUP), BF),
        pltpu.VMEM((4, 4, 2, GROUP), F32),
        pltpu.VMEM((8, 16, GROUP), BF),
        pltpu.VMEM((8, 2, GROUP), F32),
        pltpu.VMEM((4, 64, 1792), F32),
        pltpu.VMEM((2, 4, 4) + block, BF),
        pltpu.VMEM((4, 4) + block, BF),
        pltpu.VMEM((4, 4) + block, BF),
        pltpu.VMEM((16,) + block, BF),
        pltpu.VMEM((2, 4, 4) + block, BF),
        pltpu.VMEM((2, 4, 4) + block, BF),
        pltpu.VMEM((4, 4) + block, BF),
        pltpu.VMEM((4, 4) + block, BF),
        pltpu.VMEM((16,) + block, BF),
    ]
    scratch += [sem((n,)) for n in (8, 14, 14, 4, 4, 5, 5)]
    scratch += [pltpu.SemaphoreType.REGULAR, pltpu.SemaphoreType.REGULAR]
    scratch += [sem((4,))] * 4 + [sem((4, 4))] * 4 + [sem((8,))] * 4
    scratch += [sem((n,)) for n in (4, 4, 16, 16, 16, 16, 4, 4, 4, 4, 16, 16)]
    both = pl.pallas_call(
        kernel,
        out_shape=out,
        in_specs=[smem] + [vmem] * 5 + [any_spec] * 8,
        out_specs=vmem,
        scratch_shapes=scratch,
        compiler_params=pltpu.CompilerParams(
            collective_id=0, has_side_effects=True, vmem_limit_bytes=62 * 2**20
        ),
    )(
        suffix_lengths,
        hidden,
        new_latents,
        rms_gain.reshape(8, 1, HALF),
        gate_ids.T,
        gate_weights.T,
        queries.reshape(256, LATK),
        prompt_latents.T,
        jnp.swapaxes(suffix_cache, 1, 2),
        value_up,
        out_proj.reshape(512, D),
        w_gate[0],
        w_up[0],
        w_down[0],
    )
    return both[0], both[1]


def solution(mesh):
    placed = (
        P(("prompt", "resp"), "expert"),
        P(("prompt", "resp"), "expert", None),
        P(("prompt", "resp"), None),
        P(("prompt", "resp"), None, None),
        P(("prompt", "resp")),
        P(("prompt", "resp", "expert"), None),
        P("expert", None, None),
        P("expert", "resp", None),
        P(),
        P("prompt", None),
        P("prompt", None),
        P("expert", None, "resp"),
        P("expert", None, "resp"),
        P("expert", "resp", None),
    )
    return jax.shard_map(
        on_device,
        mesh=mesh,
        in_specs=placed,
        out_specs=(P(("prompt", "resp"), "expert"), P(("prompt", "resp"), "expert")),
        check_vma=False,
    )
```

```python
import jax
import jax.numpy as jnp
from jax import lax
from jax.experimental import pallas as pl
from jax.experimental.pallas import tpu as pltpu
from jax.sharding import PartitionSpec as P

MESH = pl.DeviceIdType.MESH
BF = jnp.bfloat16
F32 = jnp.float32
LAT, ROPE, LATK = 512, 64, 576
SCALE2 = (128 + 64) ** -0.5 * 1.4426950408889634
FLOOR = -0.5e30
DEAD = -1e30
D = 7168
HALF = 896
KC = 256
GROUP = 512


def iota(shape, dim):
    return lax.broadcasted_iota(jnp.int32, shape, dim)


def dot(a, b):
    return jnp.dot(a, b, preferred_element_type=F32)


def kernel(
    slen,
    hid,
    newl,
    gain,
    gids,
    gwts,
    q_in,
    k_in,
    suf_in,
    vup_in,
    wo_in,
    wg_in,
    wu_in,
    wd_in,
    out_ref,
    q_own,
    q_all,
    place,
    qt,
    kt_own,
    kt_all,
    k_own,
    k_row,
    suf,
    nl,
    acc,
    mx,
    sm,
    vup,
    wo,
    wg,
    wu,
    wd,
    ctx,
    hv,
    hv_tx,
    hv_tw,
    st_own,
    st_tw,
    z_tx,
    z_rx,
    st_z,
    a_old,
    a_buf,
    a_rx,
    a_sum,
    a_in,
    ag,
    m_buf,
    m_rx,
    m_sum,
    m_in,
    ld,
    kss,
    krs,
    qss,
    qrs,
    qcs,
    qcr,
    near,
    far,
    tws,
    twr,
    tss,
    tsr,
    zss,
    zrs,
    zts,
    ztr,
    acs,
    acr,
    ars_s,
    ars_r,
    ags_s,
    ags_r,
    agc_s,
    agc_r,
    mcs,
    mcr,
    mrs_s,
    mrs_r,
):
    e = lax.axis_index("expert")
    r = lax.axis_index("resp")
    c = lax.rem(r, 2)
    z = r // 2
    right, left = lax.rem(e + 1, 4), lax.rem(e + 3, 4)
    twin = {"resp": z * 2 + 1 - c}

    def remote(src, dst, ssem, rsem, dev):
        return pltpu.make_async_remote_copy(
            src_ref=src, dst_ref=dst, send_sem=ssem, recv_sem=rsem, device_id=dev, device_id_type=MESH
        )

    def same_core(de, dz):
        return {"expert": lax.rem(e + de, 4), "resp": lax.rem(z + dz, 4) * 2 + c}

    loads = [
        pltpu.make_async_copy(q_in, q_own, ld.at[0]),
        pltpu.make_async_copy(k_in, kt_own, ld.at[1]),
        pltpu.make_async_copy(suf_in, suf, ld.at[2]),
        pltpu.make_async_copy(vup_in, vup, ld.at[3]),
        pltpu.make_async_copy(wo_in, wo, ld.at[4]),
        pltpu.make_async_copy(wg_in, wg, ld.at[5]),
        pltpu.make_async_copy(wu_in, wu, ld.at[6]),
        pltpu.make_async_copy(wd_in, wd, ld.at[7]),
    ]
    neighbours = [same_core(1, 0), same_core(3, 0), same_core(0, 1), same_core(0, 3), twin]
    bar = pltpu.get_barrier_semaphore()
    for x in neighbours:
        pl.semaphore_signal(bar, inc=1, device_id=x, device_id_type=MESH)
    for x in loads[:3]:
        x.start()
    loads[0].wait()
    q_all[r] = q_own[...].T
    pl.semaphore_wait(bar, 5)

    def k_send(src, j, d):
        dev = {"expert": right if d == 0 else left}
        return remote(src, kt_all.at[2 * j + d], kss.at[2 * j + d], krs.at[2 * j + d], dev)

    def own_chunk(j, d):
        return k_in.at[:, pl.ds(KC * (j if d == 0 else 3 - j), KC)]

    def k_forward(j, d):
        dev = {"expert": right if d == 0 else left}
        if j == 0:
            return [k_send(kt_all.at[d], 4, d)]
        sems = (10 + d, 12 + d)
        return [
            remote(
                kt_all.at[2 + d, :, pl.ds(128 * i, 128)],
                kt_all.at[10 + d, :, pl.ds(128 * i, 128)],
                kss.at[sems[i]],
                krs.at[sems[i]],
                dev,
            )
            for i in range(2)
        ]

    k_own_sends = [k_send(own_chunk(j, d), j, d) for j in range(4) for d in range(2)]

    def q_block(dz):
        return q_all.at[lax.rem(z + dz, 4) * 2 + c]

    half_rows = (pl.ds(0, LATK // 2), pl.ds(LATK // 2, LATK // 2))

    def q_send(i):
        if i < 2:
            part = q_block(0)
        else:
            part = q_block(3 if i == 2 else 1).at[half_rows[i - 2]]
        return remote(part, part, qss.at[i], qrs.at[i], same_core(0, 1 if i % 2 == 0 else 3))

    def q_come(i):
        if i < 2:
            part = q_block(3 if i == 0 else 1)
        else:
            part = q_block(2).at[half_rows[i - 2]]
        return remote(part, part, qss.at[i], qrs.at[i], same_core(0, 1 if i % 2 == 0 else 3))

    def q_cross(i):
        if i < 3:
            part = q_block((0, 3, 1)[i])
        else:
            part = q_block(2).at[half_rows[i - 3]]
        return remote(part, part, qcs.at[i], qcr.at[i], twin)

    def q_cross_come(i):
        if i < 3:
            part = q_all.at[lax.rem(z + (0, 3, 1)[i], 4) * 2 + 1 - c]
        else:
            part = q_all.at[lax.rem(z + 2, 4) * 2 + 1 - c].at[half_rows[i - 3]]
        return remote(part, part, qcs.at[i], qcr.at[i], twin)

    for x in k_own_sends[:2]:
        x.start()
    q_send(0).start()
    q_send(1).start()
    q_cross(0).start()
    for x in k_own_sends[2:]:
        x.start()
    for x in neighbours:
        pl.semaphore_signal(near, inc=1, device_id=x, device_id_type=MESH)

    mx[...] = jnp.full_like(mx, FLOOR)
    sm[...] = jnp.zeros_like(sm)
    acc[...] = jnp.zeros_like(acc)
    nl[...] = jnp.zeros_like(nl)
    nl[0:8, :] = newl[...]

    loads[1].wait()
    k_own[...] = kt_own[...].T

    def soft(s, g, vt):
        old = mx[g]
        new = jnp.maximum(old, jnp.max(s, axis=0, keepdims=True))
        mx[g] = new
        p = jnp.exp2((s - new) * SCALE2)
        shrink = jnp.exp2((old - new) * SCALE2)
        sm[g] = sm[g] * shrink + jnp.sum(p, axis=0, keepdims=True)
        acc[g] = acc[g] * shrink + dot(vt, p.astype(BF))

    row, col = iota((GROUP, GROUP), 0), iota((GROUP, GROUP), 1)
    want = ((col // 8) % 2) * 256 + (col % 8) * 32 + col // 16
    place[...] = jnp.where(row == want, 1.0, 0.0).astype(BF)

    def make_qt(g):
        block = jnp.concatenate([q_all[2 * g], q_all[2 * g + 1]], axis=1)
        qt[g] = dot(block, place[...]).astype(BF)

    def own_keys(g):
        s0 = dot(k_own[0:GROUP, :], qt[g])
        s1 = dot(k_own[GROUP : 2 * GROUP, :], qt[g])
        soft(s0, g, kt_own[0:LAT, 0:GROUP])
        soft(s1, g, kt_own[0:LAT, GROUP : 2 * GROUP])

    q_cross_come(0).wait_recv()
    make_qt(z)
    loads[2].wait()
    for x in loads[3:]:
        x.start()
    tok = iota((1, GROUP), 1) % 16
    mine = (tok // 8) == c
    for b in range(2):
        s = dot(suf[b].T, qt[z])
        live = (iota((GROUP, GROUP), 0) < slen[b]) & mine & ((tok % 8) // 4 == b)
        soft(jnp.where(live, s, DEAD), z, suf[b, 0:LAT, :])
    s = dot(nl[...], qt[z])
    key = iota((128, GROUP), 0)
    live = (key < 8) & mine & ((tok % 8) // 4 == key // 4) & (key % 4 <= tok % 4)
    soft(jnp.where(live, s, DEAD), z, nl[:, :LAT].T)
    own_keys(z)

    for i in range(2):
        q_come(i).wait_recv()
        q_cross(i + 1).start()
        q_send(i + 2).start()
    for i in range(2):
        g = lax.rem(z + (3, 1)[i], 4)
        q_cross_come(i + 1).wait_recv()
        make_qt(g)
        own_keys(g)
    for i in range(2):
        q_come(i + 2).wait_recv()
        q_cross(i + 3).start()
    for j in range(2):
        for d in range(2):
            k_send(kt_all.at[2 * j + d], j, d).wait_recv()
            for x in k_forward(j, d):
                x.start()
    for i in range(2):
        q_cross_come(i + 3).wait_recv()
    make_qt(lax.rem(z + 2, 4))
    own_keys(lax.rem(z + 2, 4))
    pl.semaphore_wait(near, 5)
    for x in (same_core(2, 0), same_core(0, 2)):
        pl.semaphore_signal(far, inc=1, device_id=x, device_id_type=MESH)

    def arrive(j):
        for d in range(2):
            k_send(kt_all.at[2 * j + d], j, d).wait_recv()

    def keys_of(pieces):
        at = 0
        for slot, first, width in pieces:
            k_row[at : at + width] = kt_all[slot, :, first : first + width].T
            at += width
        return jnp.concatenate([kt_all[slot, 0:LAT, first : first + width] for slot, first, width in pieces], axis=1)

    def groups(count, vt):
        s = dot(k_row[0:count], qt[0])
        for g in range(4):
            nxt = dot(k_row[0:count], qt[g + 1]) if g < 3 else None
            soft(s, g, vt)
            s = nxt

    def pair(j):
        vt = keys_of([(2 * j, 0, KC), (2 * j + 1, 0, KC)])
        groups(GROUP, vt)

    def pair_last(j, carry):
        arrive(j)
        pair(j)
        return carry

    pair(0)
    pair(1)
    lax.fori_loop(2, 5, pair_last, 0)
    for d in range(2):
        k_forward(1, d)[0].wait_recv()
    groups(KC, keys_of([(10, 0, 128), (11, 0, 128)]))
    pl.semaphore_wait(far, 2)
    loads[3].wait()
    for d in range(2):
        k_forward(1, d)[1].wait_recv()
    vt = keys_of([(10, 128, 128), (11, 128, 128)])

    def lanes_of(ref, q):
        return jnp.concatenate([ref[g, :, 128 * q : 128 * q + 128] for g in range(4)], axis=1)

    def last_scores(q):
        return dot(k_row[0:KC], lanes_of(qt, q))

    def finish(q, s):
        old = lanes_of(mx, q)
        new = jnp.maximum(old, jnp.max(s, axis=0, keepdims=True))
        p = jnp.exp2((s - new) * SCALE2)
        shrink = jnp.exp2((old - new) * SCALE2)
        total = lanes_of(sm, q) * shrink + jnp.sum(p, axis=0, keepdims=True)
        part = (lanes_of(acc, q) * shrink + dot(vt, p.astype(BF))) * (1.0 / total)
        st_own[q, 0:1, :] = new
        st_own[q, 1:2, :] = total
        ctx[q] = part.astype(BF).T.reshape(4, 8, 16, LAT)
        for h in range(8):
            hv[8 * q + h] = dot(ctx[q, :, h].reshape(64, LAT), vup[8 * q + h]).reshape(4, 16, 128)
        for g in range(4):
            block = hv[8 * q : 8 * q + 8, g].reshape(128, 128).T.astype(BF).reshape(4, 2, 16, 128)
            for cc in range(2):
                hv_tx[q, cc, :, :, 128 * g : 128 * g + 128] = block[:, cc]

    def twin_sends(q):
        return [
            remote(hv_tx.at[q, 1 - c], hv_tw.at[q], tws.at[q], twr.at[q], twin),
            remote(st_own.at[q], st_tw.at[q], tss.at[q], tsr.at[q], twin),
        ]

    def z_sends(q, dz):
        to = lax.rem(z + dz, 4)
        dev = same_core(0, dz)
        return [
            remote(z_tx.at[q, to], z_rx.at[q, dz], zss.at[q, dz], zrs.at[q, dz], dev),
            remote(st_z.at[q, 0], st_z.at[q, dz], zts.at[q, dz], ztr.at[q, dz], dev),
        ]

    def weight(st, top):
        return st[1:2, :] * jnp.exp2((st[0:1, :] - top) * SCALE2)

    def chip_sum(q):
        for x in twin_sends(q):
            x.wait_recv()
        top = jnp.maximum(st_own[q, 0:1, :], st_tw[q, 0:1, :])
        w1, w2 = weight(st_own[q], top), weight(st_tw[q], top)
        inv = 1.0 / (w1 + w2)
        mine = hv_tx[q, c].astype(F32) * (w1 * inv) + hv_tw[q].astype(F32) * (w2 * inv)
        z_tx[q] = mine.astype(BF)
        st_z[q, 0, 0:1, :] = top
        st_z[q, 0, 1:2, :] = w1 + w2
        for dz in (2, 1, 3):
            for x in z_sends(q, dz):
                x.start()

    def plane_sum(q):
        for dz in (2, 1, 3):
            for x in z_sends(q, dz):
                x.wait_recv()
        top = st_z[q, 0, 0:1, :]
        for dz in range(1, 4):
            top = jnp.maximum(top, st_z[q, dz, 0:1, :])
        w = [weight(st_z[q, dz], top) for dz in range(4)]
        y = z_tx[q, z].astype(F32) * w[0]
        for dz in range(1, 4):
            y = y + z_rx[q, dz].astype(F32) * w[dz]
        return (y * (1.0 / (w[0] + w[1] + w[2] + w[3]))).astype(BF)

    s = last_scores(0)
    for q in range(4):
        nxt = last_scores(q + 1) if q < 3 else None
        finish(q, s)
        for x in twin_sends(q):
            x.start()
        if q > 0:
            chip_sum(q - 1)
        s = nxt
    chip_sum(3)

    col, row = iota((GROUP, 64), 1), iota((GROUP, 64), 0)
    want = ((row % 16) // 8) * 32 + (row // 128) * 8 + row % 8
    gather = jnp.where(col == want, 1.0, 0.0).astype(BF)
    keep = (iota((128, GROUP), 0) // 16) == ((iota((128, GROUP), 1) % 128) // 16)

    def spread(y):
        y = jnp.concatenate([y] * 8, axis=0)
        return dot(jnp.where(keep, y, jnp.zeros_like(y)), gather).T.astype(BF)

    def columns(x):
        return pl.ds(pl.multiple_of(x * 1792, 128), 1792)

    loads[4].wait()
    early = jnp.concatenate([spread(plane_sum(q)) for q in range(3)], axis=1)
    for x in range(4):
        a_old[x] = dot(early, wo[0:384, 1792 * x : 1792 * (x + 1)])
    late = spread(plane_sum(3))

    def core_send(buf, rx, ssem, rsem, x):
        return remote(buf.at[1 - c, x], rx.at[x], ssem.at[x], rsem.at[x], twin)

    def scatter_send(total_buf, landing, ssem, rsem, de, dz):
        src = total_buf.at[lax.rem(e + de, 4), lax.rem(z + dz, 4)]
        i = dz * 4 + de
        return remote(src, landing.at[i], ssem.at[i], rsem.at[i], same_core(de, dz))

    def fill(buf, x, tile):
        for cc in range(2):
            for g in range(4):
                rows = tile[32 * cc + 8 * g : 32 * cc + 8 * g + 8, :]
                buf[cc, x, g] = jnp.concatenate([rows[:, :HALF], rows[:, HALF:]], axis=0).astype(BF)

    def reduce_scatter(tile, buf, rx, total_buf, landing, cs, cr, ss, sr, meanwhile):
        def pass_on(de):
            x = lax.rem(e + de, 4)
            core_send(buf, rx, cs, cr, x).wait_recv()
            total_buf[x] = (buf[c, x].astype(F32) + rx[x].astype(F32)).astype(BF)
            for dz in (2, 1, 3, 0):
                if de or dz:
                    scatter_send(total_buf, landing, ss, sr, de, dz).start()

        last = None
        for de in (2, 1, 3, 0):
            x = lax.rem(e + de, 4)
            fill(buf, x, tile(x))
            core_send(buf, rx, cs, cr, x).start()
            if last is not None:
                pass_on(last)
            last = de
        pass_on(last)
        meanwhile()
        out = total_buf[e, z].astype(F32)
        for de in (0, 1, 3, 2):
            for dz in (0, 1, 3, 2):
                if de or dz:
                    scatter_send(total_buf, landing, ss, sr, de, dz).wait_recv()
                    out = out + landing[dz * 4 + de].astype(F32)
        return out

    def sent_first():
        for x in k_own_sends:
            x.wait_send()
        for j in range(2):
            for d in range(2):
                for x in k_forward(j, d):
                    x.wait_send()
        for i in range(4):
            q_send(i).wait_send()
        for i in range(5):
            q_cross(i).wait_send()
        for q in range(4):
            for x in twin_sends(q):
                x.wait_send()
            for dz in range(1, 4):
                for x in z_sends(q, dz):
                    x.wait_send()

    attended = reduce_scatter(
        lambda x: a_old[x] + dot(late, wo[384:512, columns(x)]), a_buf, a_rx, a_sum, a_in, acs, acr, ars_s, ars_r, sent_first
    ).astype(BF)
    hidden = jnp.concatenate([hid[:, :HALF], hid[:, HALF:]], axis=0)
    resid = (hidden.astype(F32) + attended.astype(F32)).astype(BF)
    ag[c, e, z] = resid
    out_ref[0] = jnp.concatenate([attended[0:8], attended[8:16]], axis=1)

    def ag_send(de, dz):
        i = dz * 4 + de
        return remote(ag.at[c, e, z], ag.at[c, e, z], ags_s.at[i], ags_r.at[i], same_core(de, dz))

    def ag_cross(x):
        return remote(ag.at[c, x], ag.at[c, x], agc_s.at[x], agc_r.at[x], twin)

    for de in (0, 1, 3, 2):
        for dz in (2, 1, 3, 0):
            if de or dz:
                ag_send(de, dz).start()

    loads[5].wait()
    loads[6].wait()
    squares = jnp.zeros((64, 1), F32)
    gate = jnp.zeros((64, 256), F32)
    up = jnp.zeros((64, 256), F32)
    def features(de, squares, gate, up):
        x = lax.rem(e + 4 - de, 4)
        ag_cross(x).wait_recv()
        wide = ag[:, x].astype(F32)
        for half in range(2):
            part = wide[:, :, 8 * half : 8 * half + 8, :].reshape(64, HALF)
            squares = squares + jnp.sum(part * part, axis=1, keepdims=True)
            scaled = (part * gain[2 * x + half]).astype(BF)
            rows = pl.ds(pl.multiple_of(x * 1792 + half * HALF, HALF), HALF)
            gate = gate + dot(scaled, wg[rows, :])
            up = up + dot(scaled, wu[rows, :])
        return squares, gate, up

    last = None
    for de in (0, 1, 3, 2):
        for dz in range(4):
            if de or dz:
                ag_send(de, dz).wait_recv()
        ag_cross(lax.rem(e + 4 - de, 4)).start()
        if last is not None:
            squares, gate, up = features(last, squares, gate, up)
        last = de
    squares, gate, up = features(last, squares, gate, up)
    norm = lax.rsqrt(squares * (1.0 / D) + 1e-6)
    gate = gate * norm
    up = up * norm
    act = (gate / (1.0 + jnp.exp(-gate)) * up).astype(BF)

    picked = jnp.where(gids[...] == e, gwts[...], 0.0)
    share = 2.5 * jnp.sum(picked, axis=0, keepdims=True) / jnp.sum(gwts[...], axis=0, keepdims=True)
    row, tok = iota((64, 64), 0), iota((64, 64), 1)
    here = tok == ((row // 8) % 4) * 16 + (row // 32) * 8 + row % 8
    share = jnp.sum(jnp.where(here, share, 0.0), axis=1, keepdims=True)
    loads[7].wait()
    def sent_last():
        for x in range(4):
            core_send(a_buf, a_rx, acs, acr, x).wait_send()
            ag_cross(x).wait_send()
            core_send(m_buf, m_rx, mcs, mcr, x).wait_send()
        for i in range(1, 16):
            scatter_send(a_sum, a_in, ars_s, ars_r, i % 4, i // 4).wait_send()
            ag_send(i % 4, i // 4).wait_send()
        for i in (10, 6, 14, 9, 11, 5, 7, 13, 15, 2, 8, 1, 3, 4, 12):
            scatter_send(m_sum, m_in, mrs_s, mrs_r, i % 4, i // 4).wait_send()

    moe = reduce_scatter(
        lambda x: dot(act, wd[:, columns(x)]) * share, m_buf, m_rx, m_sum, m_in, mcs, mcr, mrs_s, mrs_r, sent_last
    )
    out = (resid.astype(F32) + moe).astype(BF)
    out_ref[1] = jnp.concatenate([out[0:8], out[8:16]], axis=1)


def on_device(
    hidden,
    queries,
    new_latents,
    suffix_cache,
    suffix_lengths,
    prompt_latents,
    value_up,
    out_proj,
    rms_gain,
    gate_ids,
    gate_weights,
    w_gate,
    w_up,
    w_down,
):
    any_spec = pl.BlockSpec(memory_space=pl.ANY)
    vmem = pl.BlockSpec(memory_space=pltpu.VMEM)
    smem = pl.BlockSpec(memory_space=pltpu.SMEM)
    sem = pltpu.SemaphoreType.DMA
    out = jax.ShapeDtypeStruct((2, 8, 1792), BF)
    block = (16, HALF)
    scratch = [
        pltpu.VMEM((256, LATK), BF),
        pltpu.VMEM((8, LATK, 256), BF),
        pltpu.VMEM((GROUP, GROUP), BF),
        pltpu.VMEM((4, LATK, GROUP), BF),
        pltpu.VMEM((LATK, 1024), BF),
        pltpu.VMEM((12, LATK, KC), BF),
        pltpu.VMEM((1024, LATK), BF),
        pltpu.VMEM((GROUP, LATK), BF),
        pltpu.VMEM((2, LATK, GROUP), BF),
        pltpu.VMEM((128, LATK), BF),
        pltpu.VMEM((4, LAT, GROUP), F32),
        pltpu.VMEM((4, 1, GROUP), F32),
        pltpu.VMEM((4, 1, GROUP), F32),
        pltpu.VMEM((32, LAT, 128), BF),
        pltpu.VMEM((512, D), BF),
        pltpu.VMEM((D, 256), BF),
        pltpu.VMEM((D, 256), BF),
        pltpu.VMEM((256, D), BF),
        pltpu.VMEM((4, 4, 8, 16, LAT), BF),
        pltpu.VMEM((32, 4, 16, 128), F32),
        pltpu.VMEM((4, 2, 4, 16, GROUP), BF),
        pltpu.VMEM((4, 4, 16, GROUP), BF),
        pltpu.VMEM((4, 2, GROUP), F32),
        pltpu.VMEM((4, 2, GROUP), F32),
        pltpu.VMEM((4, 4, 16, GROUP), BF),
        pltpu.VMEM((4, 4, 16, GROUP), BF),
        pltpu.VMEM((4, 4, 2, GROUP), F32),
        pltpu.VMEM((4, 64, 1792), F32),
        pltpu.VMEM((2, 4, 4) + block, BF),
        pltpu.VMEM((4, 4) + block, BF),
        pltpu.VMEM((4, 4) + block, BF),
        pltpu.VMEM((16,) + block, BF),
        pltpu.VMEM((2, 4, 4) + block, BF),
        pltpu.VMEM((2, 4, 4) + block, BF),
        pltpu.VMEM((4, 4) + block, BF),
        pltpu.VMEM((4, 4) + block, BF),
        pltpu.VMEM((16,) + block, BF),
    ]
    scratch += [sem((n,)) for n in (8, 14, 14, 4, 4, 5, 5)]
    scratch += [pltpu.SemaphoreType.REGULAR, pltpu.SemaphoreType.REGULAR]
    scratch += [sem((4,))] * 4 + [sem((4, 4))] * 4
    scratch += [sem((n,)) for n in (4, 4, 16, 16, 16, 16, 4, 4, 4, 4, 16, 16)]
    both = pl.pallas_call(
        kernel,
        out_shape=out,
        in_specs=[smem] + [vmem] * 5 + [any_spec] * 8,
        out_specs=vmem,
        scratch_shapes=scratch,
        compiler_params=pltpu.CompilerParams(
            collective_id=0, has_side_effects=True, vmem_limit_bytes=62 * 2**20
        ),
    )(
        suffix_lengths,
        hidden,
        new_latents,
        rms_gain.reshape(8, 1, HALF),
        gate_ids.T,
        gate_weights.T,
        queries.reshape(256, LATK),
        prompt_latents.T,
        jnp.swapaxes(suffix_cache, 1, 2),
        value_up,
        out_proj.reshape(512, D),
        w_gate[0],
        w_up[0],
        w_down[0],
    )
    return both[0], both[1]


def solution(mesh):
    placed = (
        P(("prompt", "resp"), "expert"),
        P(("prompt", "resp"), "expert", None),
        P(("prompt", "resp"), None),
        P(("prompt", "resp"), None, None),
        P(("prompt", "resp")),
        P(("prompt", "resp", "expert"), None),
        P("expert", None, None),
        P("expert", "resp", None),
        P(),
        P("prompt", None),
        P("prompt", None),
        P("expert", None, "resp"),
        P("expert", None, "resp"),
        P("expert", "resp", None),
    )
    return jax.shard_map(
        on_device,
        mesh=mesh,
        in_specs=placed,
        out_specs=(P(("prompt", "resp"), "expert"), P(("prompt", "resp"), "expert")),
        check_vma=False,
    )
```

```python
import jax
import jax.numpy as jnp
from jax import lax
from jax.experimental import pallas as pl
from jax.experimental.pallas import tpu as pltpu
from jax.sharding import PartitionSpec as P

MESH = pl.DeviceIdType.MESH
BF = jnp.bfloat16
F32 = jnp.float32
LAT, ROPE, LATK = 512, 64, 576
SCALE2 = (128 + 64) ** -0.5 * 1.4426950408889634
FLOOR = -0.5e30
DEAD = -1e30
D = 7168
HALF = 896
KC = 256
GROUP = 512


def iota(shape, dim):
    return lax.broadcasted_iota(jnp.int32, shape, dim)


def dot(a, b):
    return jnp.dot(a, b, preferred_element_type=F32)


def kernel(
    slen,
    hid,
    newl,
    gain,
    gids,
    gwts,
    q_in,
    k_in,
    suf_in,
    vup_in,
    wo_in,
    wg_in,
    wu_in,
    wd_in,
    out_ref,
    q_own,
    q_all,
    place,
    qt,
    kt_own,
    kt_all,
    k_own,
    k_row,
    suf,
    nl,
    acc,
    mx,
    sm,
    vup,
    wo,
    wg,
    wu,
    wd,
    ctx,
    hv,
    hv_tx,
    hv_tw,
    st_own,
    st_tw,
    z_tx,
    z_rx,
    st_z,
    a_old,
    a_buf,
    a_rx,
    a_sum,
    a_in,
    ag,
    m_buf,
    m_rx,
    m_sum,
    m_in,
    ld,
    kss,
    krs,
    qss,
    qrs,
    qcs,
    qcr,
    near,
    far,
    tws,
    twr,
    tss,
    tsr,
    zss,
    zrs,
    zts,
    ztr,
    acs,
    acr,
    ars_s,
    ars_r,
    ags_s,
    ags_r,
    agc_s,
    agc_r,
    mcs,
    mcr,
    mrs_s,
    mrs_r,
):
    e = lax.axis_index("expert")
    r = lax.axis_index("resp")
    c = lax.rem(r, 2)
    z = r // 2
    right, left = lax.rem(e + 1, 4), lax.rem(e + 3, 4)
    twin = {"resp": z * 2 + 1 - c}

    def remote(src, dst, ssem, rsem, dev):
        return pltpu.make_async_remote_copy(
            src_ref=src, dst_ref=dst, send_sem=ssem, recv_sem=rsem, device_id=dev, device_id_type=MESH
        )

    def same_core(de, dz):
        return {"expert": lax.rem(e + de, 4), "resp": lax.rem(z + dz, 4) * 2 + c}

    loads = [
        pltpu.make_async_copy(q_in, q_own, ld.at[0]),
        pltpu.make_async_copy(k_in, kt_own, ld.at[1]),
        pltpu.make_async_copy(suf_in, suf, ld.at[2]),
        pltpu.make_async_copy(vup_in, vup, ld.at[3]),
        pltpu.make_async_copy(wo_in, wo, ld.at[4]),
        pltpu.make_async_copy(wg_in, wg, ld.at[5]),
        pltpu.make_async_copy(wu_in, wu, ld.at[6]),
        pltpu.make_async_copy(wd_in, wd, ld.at[7]),
    ]
    neighbours = [same_core(1, 0), same_core(3, 0), same_core(0, 1), same_core(0, 3), twin]
    bar = pltpu.get_barrier_semaphore()
    for x in neighbours:
        pl.semaphore_signal(bar, inc=1, device_id=x, device_id_type=MESH)
    for x in loads[:3]:
        x.start()
    loads[0].wait()
    q_all[r] = q_own[...].T
    pl.semaphore_wait(bar, 5)

    def k_send(src, j, d):
        dev = {"expert": right if d == 0 else left}
        return remote(src, kt_all.at[2 * j + d], kss.at[2 * j + d], krs.at[2 * j + d], dev)

    def own_chunk(j, d):
        return k_in.at[:, pl.ds(KC * (j if d == 0 else 3 - j), KC)]

    def k_forward(j, d):
        dev = {"expert": right if d == 0 else left}
        if j == 0:
            return [k_send(kt_all.at[d], 4, d)]
        sems = (10 + d, 12 + d)
        return [
            remote(
                kt_all.at[2 + d, :, pl.ds(128 * i, 128)],
                kt_all.at[10 + d, :, pl.ds(128 * i, 128)],
                kss.at[sems[i]],
                krs.at[sems[i]],
                dev,
            )
            for i in range(2)
        ]

    k_own_sends = [k_send(own_chunk(j, d), j, d) for j in range(4) for d in range(2)]

    def q_block(dz):
        return q_all.at[lax.rem(z + dz, 4) * 2 + c]

    half_rows = (pl.ds(0, LATK // 2), pl.ds(LATK // 2, LATK // 2))

    def q_send(i):
        if i < 2:
            part = q_block(0)
        else:
            part = q_block(3 if i == 2 else 1).at[half_rows[i - 2]]
        return remote(part, part, qss.at[i], qrs.at[i], same_core(0, 1 if i % 2 == 0 else 3))

    def q_come(i):
        if i < 2:
            part = q_block(3 if i == 0 else 1)
        else:
            part = q_block(2).at[half_rows[i - 2]]
        return remote(part, part, qss.at[i], qrs.at[i], same_core(0, 1 if i % 2 == 0 else 3))

    def q_cross(i):
        if i < 3:
            part = q_block((0, 3, 1)[i])
        else:
            part = q_block(2).at[half_rows[i - 3]]
        return remote(part, part, qcs.at[i], qcr.at[i], twin)

    def q_cross_come(i):
        if i < 3:
            part = q_all.at[lax.rem(z + (0, 3, 1)[i], 4) * 2 + 1 - c]
        else:
            part = q_all.at[lax.rem(z + 2, 4) * 2 + 1 - c].at[half_rows[i - 3]]
        return remote(part, part, qcs.at[i], qcr.at[i], twin)

    for x in k_own_sends[:2]:
        x.start()
    q_send(0).start()
    q_send(1).start()
    q_cross(0).start()
    for x in k_own_sends[2:]:
        x.start()
    for x in neighbours:
        pl.semaphore_signal(near, inc=1, device_id=x, device_id_type=MESH)

    mx[...] = jnp.full_like(mx, FLOOR)
    sm[...] = jnp.zeros_like(sm)
    acc[...] = jnp.zeros_like(acc)
    nl[...] = jnp.zeros_like(nl)
    nl[0:8, :] = newl[...]

    loads[1].wait()
    k_own[...] = kt_own[...].T

    def soft(s, g, vt):
        old = mx[g]
        new = jnp.maximum(old, jnp.max(s, axis=0, keepdims=True))
        mx[g] = new
        p = jnp.exp2((s - new) * SCALE2)
        shrink = jnp.exp2((old - new) * SCALE2)
        sm[g] = sm[g] * shrink + jnp.sum(p, axis=0, keepdims=True)
        acc[g] = acc[g] * shrink + dot(vt, p.astype(BF))

    row, col = iota((GROUP, GROUP), 0), iota((GROUP, GROUP), 1)
    want = ((col // 8) % 2) * 256 + (col % 8) * 32 + col // 16
    place[...] = jnp.where(row == want, 1.0, 0.0).astype(BF)

    def make_qt(g):
        block = jnp.concatenate([q_all[2 * g], q_all[2 * g + 1]], axis=1)
        qt[g] = dot(block, place[...]).astype(BF)

    def own_keys(g):
        s0 = dot(k_own[0:GROUP, :], qt[g])
        s1 = dot(k_own[GROUP : 2 * GROUP, :], qt[g])
        soft(s0, g, kt_own[0:LAT, 0:GROUP])
        soft(s1, g, kt_own[0:LAT, GROUP : 2 * GROUP])

    q_cross_come(0).wait_recv()
    make_qt(z)
    loads[2].wait()
    for x in loads[3:]:
        x.start()
    tok = iota((1, GROUP), 1) % 16
    mine = (tok // 8) == c
    for b in range(2):
        s = dot(suf[b].T, qt[z])
        live = (iota((GROUP, GROUP), 0) < slen[b]) & mine & ((tok % 8) // 4 == b)
        soft(jnp.where(live, s, DEAD), z, suf[b, 0:LAT, :])
    s = dot(nl[...], qt[z])
    key = iota((128, GROUP), 0)
    live = (key < 8) & mine & ((tok % 8) // 4 == key // 4) & (key % 4 <= tok % 4)
    soft(jnp.where(live, s, DEAD), z, nl[:, :LAT].T)
    own_keys(z)

    for i in range(2):
        q_come(i).wait_recv()
        q_cross(i + 1).start()
        q_send(i + 2).start()
    for i in range(2):
        g = lax.rem(z + (3, 1)[i], 4)
        q_cross_come(i + 1).wait_recv()
        make_qt(g)
        own_keys(g)
    for i in range(2):
        q_come(i + 2).wait_recv()
        q_cross(i + 3).start()
    for j in range(2):
        for d in range(2):
            k_send(kt_all.at[2 * j + d], j, d).wait_recv()
            for x in k_forward(j, d):
                x.start()
    for i in range(2):
        q_cross_come(i + 3).wait_recv()
    make_qt(lax.rem(z + 2, 4))
    own_keys(lax.rem(z + 2, 4))
    pl.semaphore_wait(near, 5)
    for x in (same_core(2, 0), same_core(0, 2)):
        pl.semaphore_signal(far, inc=1, device_id=x, device_id_type=MESH)

    def arrive(j):
        for d in range(2):
            k_send(kt_all.at[2 * j + d], j, d).wait_recv()

    def keys_of(pieces):
        at = 0
        for slot, first, width in pieces:
            k_row[at : at + width] = kt_all[slot, :, first : first + width].T
            at += width
        return jnp.concatenate([kt_all[slot, 0:LAT, first : first + width] for slot, first, width in pieces], axis=1)

    def groups(count, vt):
        s = dot(k_row[0:count], qt[0])
        for g in range(4):
            nxt = dot(k_row[0:count], qt[g + 1]) if g < 3 else None
            soft(s, g, vt)
            s = nxt

    def pair(j):
        vt = keys_of([(2 * j, 0, KC), (2 * j + 1, 0, KC)])
        groups(GROUP, vt)

    def pair_last(j, carry):
        arrive(j)
        pair(j)
        return carry

    pair(0)
    pair(1)
    lax.fori_loop(2, 5, pair_last, 0)
    for d in range(2):
        k_forward(1, d)[0].wait_recv()
    groups(KC, keys_of([(10, 0, 128), (11, 0, 128)]))
    pl.semaphore_wait(far, 2)
    loads[3].wait()
    for d in range(2):
        k_forward(1, d)[1].wait_recv()
    vt = keys_of([(10, 128, 128), (11, 128, 128)])

    def lanes_of(ref, q):
        return jnp.concatenate([ref[g, :, 128 * q : 128 * q + 128] for g in range(4)], axis=1)

    def last_scores(q):
        return dot(k_row[0:KC], lanes_of(qt, q))

    def finish(q, s):
        old = lanes_of(mx, q)
        new = jnp.maximum(old, jnp.max(s, axis=0, keepdims=True))
        p = jnp.exp2((s - new) * SCALE2)
        shrink = jnp.exp2((old - new) * SCALE2)
        total = lanes_of(sm, q) * shrink + jnp.sum(p, axis=0, keepdims=True)
        part = (lanes_of(acc, q) * shrink + dot(vt, p.astype(BF))) * (1.0 / total)
        st_own[q, 0:1, :] = new
        st_own[q, 1:2, :] = total
        ctx[q] = part.astype(BF).T.reshape(4, 8, 16, LAT)
        for h in range(8):
            hv[8 * q + h] = dot(ctx[q, :, h].reshape(64, LAT), vup[8 * q + h]).reshape(4, 16, 128)
        for g in range(4):
            block = hv[8 * q : 8 * q + 8, g].reshape(128, 128).T.astype(BF).reshape(4, 2, 16, 128)
            for cc in range(2):
                hv_tx[q, cc, :, :, 128 * g : 128 * g + 128] = block[:, cc]

    def twin_sends(q):
        return [
            remote(hv_tx.at[q, 1 - c], hv_tw.at[q], tws.at[q], twr.at[q], twin),
            remote(st_own.at[q], st_tw.at[q], tss.at[q], tsr.at[q], twin),
        ]

    def z_sends(q, dz):
        to = lax.rem(z + dz, 4)
        dev = same_core(0, dz)
        return [
            remote(z_tx.at[q, to], z_rx.at[q, dz], zss.at[q, dz], zrs.at[q, dz], dev),
            remote(st_z.at[q, 0], st_z.at[q, dz], zts.at[q, dz], ztr.at[q, dz], dev),
        ]

    def weight(st, top):
        return st[1:2, :] * jnp.exp2((st[0:1, :] - top) * SCALE2)

    def chip_sum(q):
        for x in twin_sends(q):
            x.wait_recv()
        top = jnp.maximum(st_own[q, 0:1, :], st_tw[q, 0:1, :])
        w1, w2 = weight(st_own[q], top), weight(st_tw[q], top)
        inv = 1.0 / (w1 + w2)
        mine = hv_tx[q, c].astype(F32) * (w1 * inv) + hv_tw[q].astype(F32) * (w2 * inv)
        z_tx[q] = mine.astype(BF)
        st_z[q, 0, 0:1, :] = top
        st_z[q, 0, 1:2, :] = w1 + w2
        for dz in (2, 1, 3):
            for x in z_sends(q, dz):
                x.start()

    def plane_sum(q):
        for dz in (2, 1, 3):
            for x in z_sends(q, dz):
                x.wait_recv()
        top = st_z[q, 0, 0:1, :]
        for dz in range(1, 4):
            top = jnp.maximum(top, st_z[q, dz, 0:1, :])
        w = [weight(st_z[q, dz], top) for dz in range(4)]
        y = z_tx[q, z].astype(F32) * w[0]
        for dz in range(1, 4):
            y = y + z_rx[q, dz].astype(F32) * w[dz]
        return (y * (1.0 / (w[0] + w[1] + w[2] + w[3]))).astype(BF)

    s = last_scores(0)
    for q in range(4):
        nxt = last_scores(q + 1) if q < 3 else None
        finish(q, s)
        for x in twin_sends(q):
            x.start()
        if q > 0:
            chip_sum(q - 1)
        s = nxt
    chip_sum(3)

    col, row = iota((GROUP, 64), 1), iota((GROUP, 64), 0)
    want = ((row % 16) // 8) * 32 + (row // 128) * 8 + row % 8
    gather = jnp.where(col == want, 1.0, 0.0).astype(BF)
    keep = (iota((128, GROUP), 0) // 16) == ((iota((128, GROUP), 1) % 128) // 16)

    def spread(y):
        y = jnp.concatenate([y] * 8, axis=0)
        return dot(jnp.where(keep, y, jnp.zeros_like(y)), gather).T.astype(BF)

    def columns(x):
        return pl.ds(pl.multiple_of(x * 1792, 128), 1792)

    loads[4].wait()
    early = jnp.concatenate([spread(plane_sum(q)) for q in range(3)], axis=1)
    for x in range(4):
        a_old[x] = dot(early, wo[0:384, 1792 * x : 1792 * (x + 1)])
    late = spread(plane_sum(3))

    def core_send(buf, rx, ssem, rsem, x):
        return remote(buf.at[1 - c, x], rx.at[x], ssem.at[x], rsem.at[x], twin)

    def scatter_send(total_buf, landing, ssem, rsem, de, dz):
        src = total_buf.at[lax.rem(e + de, 4), lax.rem(z + dz, 4)]
        i = dz * 4 + de
        return remote(src, landing.at[i], ssem.at[i], rsem.at[i], same_core(de, dz))

    def fill(buf, x, tile):
        for cc in range(2):
            for g in range(4):
                rows = tile[32 * cc + 8 * g : 32 * cc + 8 * g + 8, :]
                buf[cc, x, g] = jnp.concatenate([rows[:, :HALF], rows[:, HALF:]], axis=0).astype(BF)

    def reduce_scatter(tile, buf, rx, total_buf, landing, cs, cr, ss, sr, meanwhile):
        def pass_on(de):
            x = lax.rem(e + de, 4)
            core_send(buf, rx, cs, cr, x).wait_recv()
            total_buf[x] = (buf[c, x].astype(F32) + rx[x].astype(F32)).astype(BF)
            for dz in (2, 1, 3, 0):
                if de or dz:
                    scatter_send(total_buf, landing, ss, sr, de, dz).start()

        last = None
        for de in (2, 1, 3, 0):
            x = lax.rem(e + de, 4)
            fill(buf, x, tile(x))
            core_send(buf, rx, cs, cr, x).start()
            if last is not None:
                pass_on(last)
            last = de
        pass_on(last)
        meanwhile()
        out = total_buf[e, z].astype(F32)
        for de in (0, 1, 3, 2):
            for dz in (0, 1, 3, 2):
                if de or dz:
                    scatter_send(total_buf, landing, ss, sr, de, dz).wait_recv()
                    out = out + landing[dz * 4 + de].astype(F32)
        return out

    def sent_first():
        for x in k_own_sends:
            x.wait_send()
        for j in range(2):
            for d in range(2):
                for x in k_forward(j, d):
                    x.wait_send()
        for i in range(4):
            q_send(i).wait_send()
        for i in range(5):
            q_cross(i).wait_send()
        for q in range(4):
            for x in twin_sends(q):
                x.wait_send()
            for dz in range(1, 4):
                for x in z_sends(q, dz):
                    x.wait_send()

    attended = reduce_scatter(
        lambda x: a_old[x] + dot(late, wo[384:512, columns(x)]), a_buf, a_rx, a_sum, a_in, acs, acr, ars_s, ars_r, sent_first
    ).astype(BF)
    hidden = jnp.concatenate([hid[:, :HALF], hid[:, HALF:]], axis=0)
    resid = (hidden.astype(F32) + attended.astype(F32)).astype(BF)
    ag[c, e, z] = resid

    def ag_send(de, dz):
        i = dz * 4 + de
        return remote(ag.at[c, e, z], ag.at[c, e, z], ags_s.at[i], ags_r.at[i], same_core(de, dz))

    def ag_cross(x):
        return remote(ag.at[c, x], ag.at[c, x], agc_s.at[x], agc_r.at[x], twin)

    for de in (0, 1, 3, 2):
        for dz in (2, 1, 3, 0):
            if de or dz:
                ag_send(de, dz).start()

    out_ref[0] = jnp.concatenate([attended[0:8], attended[8:16]], axis=1)
    picked = jnp.where(gids[...] == e, gwts[...], 0.0)
    share = 2.5 * jnp.sum(picked, axis=0, keepdims=True) / jnp.sum(gwts[...], axis=0, keepdims=True)
    row, tok = iota((64, 64), 0), iota((64, 64), 1)
    here = tok == ((row // 8) % 4) * 16 + (row // 32) * 8 + row % 8
    share = jnp.sum(jnp.where(here, share, 0.0), axis=1, keepdims=True)
    loads[5].wait()
    loads[6].wait()
    loads[7].wait()
    squares = jnp.zeros((64, 1), F32)
    gate = jnp.zeros((64, 256), F32)
    up = jnp.zeros((64, 256), F32)
    def features(de, squares, gate, up):
        x = lax.rem(e + 4 - de, 4)
        ag_cross(x).wait_recv()
        wide = ag[:, x].astype(F32)
        for half in range(2):
            part = wide[:, :, 8 * half : 8 * half + 8, :].reshape(64, HALF)
            squares = squares + jnp.sum(part * part, axis=1, keepdims=True)
            scaled = (part * gain[2 * x + half]).astype(BF)
            rows = pl.ds(pl.multiple_of(x * 1792 + half * HALF, HALF), HALF)
            gate = gate + dot(scaled, wg[rows, :])
            up = up + dot(scaled, wu[rows, :])
        return squares, gate, up

    last = None
    for de in (0, 1, 3, 2):
        for dz in range(4):
            if de or dz:
                ag_send(de, dz).wait_recv()
        ag_cross(lax.rem(e + 4 - de, 4)).start()
        if last is not None:
            squares, gate, up = features(last, squares, gate, up)
        last = de
    squares, gate, up = features(last, squares, gate, up)
    norm = lax.rsqrt(squares * (1.0 / D) + 1e-6)
    gate = gate * norm
    up = up * norm
    act = (gate / (1.0 + jnp.exp(-gate)) * up).astype(BF)

    def sent_last():
        for x in range(4):
            core_send(a_buf, a_rx, acs, acr, x).wait_send()
            ag_cross(x).wait_send()
            core_send(m_buf, m_rx, mcs, mcr, x).wait_send()
        for i in range(1, 16):
            scatter_send(a_sum, a_in, ars_s, ars_r, i % 4, i // 4).wait_send()
            ag_send(i % 4, i // 4).wait_send()
        for i in (10, 6, 14, 9, 11, 5, 7, 13, 15, 2, 8, 1, 3, 4, 12):
            scatter_send(m_sum, m_in, mrs_s, mrs_r, i % 4, i // 4).wait_send()

    moe = reduce_scatter(
        lambda x: dot(act, wd[:, columns(x)]) * share, m_buf, m_rx, m_sum, m_in, mcs, mcr, mrs_s, mrs_r, sent_last
    )
    out = (resid.astype(F32) + moe).astype(BF)
    out_ref[1] = jnp.concatenate([out[0:8], out[8:16]], axis=1)


def on_device(
    hidden,
    queries,
    new_latents,
    suffix_cache,
    suffix_lengths,
    prompt_latents,
    value_up,
    out_proj,
    rms_gain,
    gate_ids,
    gate_weights,
    w_gate,
    w_up,
    w_down,
):
    any_spec = pl.BlockSpec(memory_space=pl.ANY)
    vmem = pl.BlockSpec(memory_space=pltpu.VMEM)
    smem = pl.BlockSpec(memory_space=pltpu.SMEM)
    sem = pltpu.SemaphoreType.DMA
    out = jax.ShapeDtypeStruct((2, 8, 1792), BF)
    block = (16, HALF)
    scratch = [
        pltpu.VMEM((256, LATK), BF),
        pltpu.VMEM((8, LATK, 256), BF),
        pltpu.VMEM((GROUP, GROUP), BF),
        pltpu.VMEM((4, LATK, GROUP), BF),
        pltpu.VMEM((LATK, 1024), BF),
        pltpu.VMEM((12, LATK, KC), BF),
        pltpu.VMEM((1024, LATK), BF),
        pltpu.VMEM((GROUP, LATK), BF),
        pltpu.VMEM((2, LATK, GROUP), BF),
        pltpu.VMEM((128, LATK), BF),
        pltpu.VMEM((4, LAT, GROUP), F32),
        pltpu.VMEM((4, 1, GROUP), F32),
        pltpu.VMEM((4, 1, GROUP), F32),
        pltpu.VMEM((32, LAT, 128), BF),
        pltpu.VMEM((512, D), BF),
        pltpu.VMEM((D, 256), BF),
        pltpu.VMEM((D, 256), BF),
        pltpu.VMEM((256, D), BF),
        pltpu.VMEM((4, 4, 8, 16, LAT), BF),
        pltpu.VMEM((32, 4, 16, 128), F32),
        pltpu.VMEM((4, 2, 4, 16, GROUP), BF),
        pltpu.VMEM((4, 4, 16, GROUP), BF),
        pltpu.VMEM((4, 2, GROUP), F32),
        pltpu.VMEM((4, 2, GROUP), F32),
        pltpu.VMEM((4, 4, 16, GROUP), BF),
        pltpu.VMEM((4, 4, 16, GROUP), BF),
        pltpu.VMEM((4, 4, 2, GROUP), F32),
        pltpu.VMEM((4, 64, 1792), F32),
        pltpu.VMEM((2, 4, 4) + block, BF),
        pltpu.VMEM((4, 4) + block, BF),
        pltpu.VMEM((4, 4) + block, BF),
        pltpu.VMEM((16,) + block, BF),
        pltpu.VMEM((2, 4, 4) + block, BF),
        pltpu.VMEM((2, 4, 4) + block, BF),
        pltpu.VMEM((4, 4) + block, BF),
        pltpu.VMEM((4, 4) + block, BF),
        pltpu.VMEM((16,) + block, BF),
    ]
    scratch += [sem((n,)) for n in (8, 14, 14, 4, 4, 5, 5)]
    scratch += [pltpu.SemaphoreType.REGULAR, pltpu.SemaphoreType.REGULAR]
    scratch += [sem((4,))] * 4 + [sem((4, 4))] * 4
    scratch += [sem((n,)) for n in (4, 4, 16, 16, 16, 16, 4, 4, 4, 4, 16, 16)]
    both = pl.pallas_call(
        kernel,
        out_shape=out,
        in_specs=[smem] + [vmem] * 5 + [any_spec] * 8,
        out_specs=vmem,
        scratch_shapes=scratch,
        compiler_params=pltpu.CompilerParams(
            collective_id=0, has_side_effects=True, vmem_limit_bytes=62 * 2**20
        ),
    )(
        suffix_lengths,
        hidden,
        new_latents,
        rms_gain.reshape(8, 1, HALF),
        gate_ids.T,
        gate_weights.T,
        queries.reshape(256, LATK),
        prompt_latents.T,
        jnp.swapaxes(suffix_cache, 1, 2),
        value_up,
        out_proj.reshape(512, D),
        w_gate[0],
        w_up[0],
        w_down[0],
    )
    return both[0], both[1]


def solution(mesh):
    placed = (
        P(("prompt", "resp"), "expert"),
        P(("prompt", "resp"), "expert", None),
        P(("prompt", "resp"), None),
        P(("prompt", "resp"), None, None),
        P(("prompt", "resp")),
        P(("prompt", "resp", "expert"), None),
        P("expert", None, None),
        P("expert", "resp", None),
        P(),
        P("prompt", None),
        P("prompt", None),
        P("expert", None, "resp"),
        P("expert", None, "resp"),
        P("expert", "resp", None),
    )
    return jax.shard_map(
        on_device,
        mesh=mesh,
        in_specs=placed,
        out_specs=(P(("prompt", "resp"), "expert"), P(("prompt", "resp"), "expert")),
        check_vma=False,
    )
```
